32 devices in a mesh: outer: 2 (over x), role: 16 (over z, y, core).
Axes of the slice: x: 2, y: 2, z: 4, core: 2. Of those that a mesh axis runs over, the one named last changes fastest.
Arguments:
- images: bfloat16 [512, 5120], P(('outer', 'role')), parts along dimension 0, may hold values from -6 to 6
- vis_gain: float32 [5120], replicated, may hold values from 0.25 to 1.75
- w_merge: bfloat16 [5120, 8192], P(None, 'role'), may hold values from -0.078125 to 0.078125
- prompt_text: bfloat16 [7680, 8192], P(('outer', 'role')), parts along dimension 0, may hold values from -6 to 6
- norm_gain: float32 [8192], replicated, may hold values from 0.25 to 1.75
- w_kv: bfloat16 [8192, 2048], P('role'), may hold values from -0.0625 to 0.0625
- new_query: bfloat16 [32, 8192], P(('outer', 'role')), parts along dimension 0
- new_kv: bfloat16 [32, 2048], P(('outer', 'role')), parts along dimension 0
- text_len: int32 [32], P(('outer', 'role')), parts along dimension 0, may hold values from 1 to 240
- img_count: int32 [64], P(('outer', 'role')), parts along dimension 0, may hold values from 1 to 8
- img_dest: int32 [64, 1], P(('outer', 'role')), parts along dimension 0, may hold values from 0 to 15; in each aligned block of 32 rows (0 to 31, 32 to 63, ...) at most 4 rows name the same one
- block_dest: int32 [544, 1], P(('outer', 'role')), parts along dimension 0, may hold values from 0 to 15; in each aligned block of 17 rows (0 to 16, 17 to 33, ...) at most 2 rows name the same one
- past_cache: bfloat16 [1024, 16, 2048], P(('outer', 'role')), parts along dimension 0, may hold values from -6 to 6
- past_scale: bfloat16 [1024, 16], P(('outer', 'role')), parts along dimension 0, may hold values from 0.5 to 2
- past_owner: int32 [1024, 1], P(('outer', 'role')), parts along dimension 0, may hold values from 0 to 15; in each aligned block of 32 rows (0 to 31, 32 to 63, ...) at most 4 rows name the same one
Outputs:
- kv_cache: bfloat16 [1024, 16, 2048], P(('outer', 'role')), parts along dimension 0
- cache_scale: bfloat16 [1024, 16], P(('outer', 'role')), parts along dimension 0
- attended: bfloat16 [32, 8192], P(('outer', 'role')), parts along dimension 0
The draws below stay inside these ranges and needn't reach their ends.
There are 2 independent parts, one for each index of `outer`. The reference program is written for one: setup_inputs(seed, part) draws one part's arguments, and reference() takes and returns one part's arrays. A program takes and returns all parts, laid end to end along the dimension named above; an argument that names none is the same for every part. Nothing has to cross between parts.
Inputs may be any that keep to these rules, and one draw needn't show every extreme that they name: `img_dest`: every prompt has one image or more and no prompt has more than 4; some prompt has exactly 4. `block_dest`: of one prompt's 17 blocks no rank takes more than 2; some rank takes exactly 2. `past_owner`: every request owns one earlier page or more.
All inputs are finite; a program needn't handle non-finite values.
Results may differ from the reference program's by a relative error of at most 0.0085.
Values may be sent and summed in bfloat16 or wider, within the bound.
A program may use at most 128 MiB of HBM per device.

```python
import math
import jax
import jax.numpy as jnp
import numpy as np
from jax import lax

D = 8192
VIS = 5120
H = 64
KVH = 8
HD = 128
IMG_TOK = 8
IMGCAP = 4
TEXT = 240
BLK = 16
PASTP = 32
NB = 17
CAPB = 2
PAGES = 32
PROMPTS = 16
IMAGES = 32
N_ROLE = 16


def fresh_pair(key):
    return jax.random.normal(key, (PROMPTS, 2 * KVH * HD), jnp.float32)


def draw_new_kv(key, part):
    values = fresh_pair(key)
    return values.astype(jnp.bfloat16)


def draw_new_query(key, part):
    key = jax.random.fold_in(key, 5)
    first_key = jax.random.fold_in(key, 0)
    groups = H // KVH
    base = jax.random.normal(first_key, (PROMPTS, KVH, groups, HD), jnp.float32)
    return base.reshape(PROMPTS, H * HD).astype(jnp.bfloat16)


def draw_text_len(key, part):
    key = jax.random.fold_in(key, 7)
    values = jax.random.randint(key, (PROMPTS,), 1, TEXT + 1)
    return values.at[0].set(TEXT).astype(jnp.int32)


def draw_img_count(key, part):
    key = jax.random.fold_in(key, 11)
    values = jax.random.randint(key, (IMAGES,), 1, IMG_TOK + 1)
    return values.at[0].set(IMG_TOK).astype(jnp.int32)


def shard_levels(own_key, shape, cuts, least, top_value):
    factor_of = 1.0
    for dim, blocks in cuts:
        draws = jax.random.uniform(jax.random.fold_in(jax.random.fold_in(own_key, 6), dim), (blocks,), jnp.float32, least / len(cuts), top_value / len(cuts))
        factor_of = factor_of * jnp.repeat(jnp.exp(draws), shape[dim] // blocks).reshape((-1,) + (1,) * (len(shape) - 1 - dim))
    return factor_of


def routed_block(stream_key, own, number, rows, number_of, top, most, lean):
    ranking = jax.random.permutation(stream_key, number_of)
    packed, ordinary = portions_of(number_of, rows * top, most, lean, True), portions_of(number_of, rows * top, most, lean, False)
    places = jnp.arange(number_of)

    def named(tallies, offset_by):
        used = int((tallies > 0).sum())
        fixed = max(1, used // 4)
        passed = fixed + (places - fixed + offset_by * (used - fixed)) % max(1, number_of - fixed)
        return jnp.zeros((number_of,), jnp.int32).at[ranking[jnp.where(places < fixed, places, passed)]].set(jnp.asarray(tallies, jnp.int32))

    tallies = jnp.where(number % 4 == 0, named(packed, number // 4), named(ordinary, number - number // 4 - 1))
    mixed = jax.random.permutation(jax.random.fold_in(own, 3), number_of)
    source_of, taker = mixed[0:number_of // 2 * 2:2], mixed[1:number_of // 2 * 2:2]
    room = jnp.minimum(tallies[source_of] - 1, most - tallies[taker]) // 2
    room = jnp.where((source_of == ranking[0]) | (taker == ranking[0]) | (tallies[taker] == 0), 0, jnp.maximum(room, 0))
    passed = jax.random.randint(jax.random.fold_in(own, 4), (number_of // 2,), 0, 1 << 20) % (room + 1)
    tallies = tallies.at[source_of].add(-passed).at[taker].add(passed)
    members = jnp.searchsorted(jnp.cumsum(tallies), jnp.arange(rows * top), side="right").astype(jnp.int32)
    listing = members.reshape(top, rows).T
    listing = listing[jax.random.permutation(jax.random.fold_in(own, 1), rows)]
    offset_by = jax.random.randint(jax.random.fold_in(own, 2), (rows, 1), 0, top)
    return jnp.take_along_axis(listing, (jnp.arange(top)[None, :] + offset_by) % top, axis=1)


def portions_of(count, total, bound, lean, full):
    loads = [(1 << 20) // math.isqrt(standing ** lean) + 1 for standing in range(1, count + 1)]
    largest = bound if full else min(bound, max(-(-total // count), total * loads[0] // sum(loads)))
    least = 1 if total - largest >= count - 1 else 0
    counts, rest = [largest] + [least] * (count - 1), total - largest - least * (count - 1)
    while rest > 0:
        free = [i for i in range(1, count) if counts[i] < largest] or [i for i in range(1, count) if counts[i] < bound]
        mass, budget = sum([loads[i] for i in free]), rest
        for i in free:
            extra = min(bound - counts[i], max(1, budget * loads[i] // mass), rest)
            counts[i] = counts[i] + extra
            rest = rest - extra
    return np.array(counts)


def scatter_about(rng, shape, spread, reach, cuts=(), kind=jnp.bfloat16):
    array = spread * jax.random.normal(rng, shape, jnp.float32)
    if cuts:
        array = array * shard_levels(rng, shape, cuts, -0.22, 0.18)
    return jnp.clip(array, -reach, reach).astype(kind)


def setup_inputs(seed: int = 0, part: int = 0) -> dict:
    splits = jax.random.split(jax.random.key(seed), 16)
    part_splits = jax.random.split(jax.random.fold_in(splits[15], part), 16)
    images = scatter_about(part_splits[0], (IMAGES * IMG_TOK, VIS), 1.0, 6.0, ((0, 16),))
    vis_gain = jnp.clip(1.0 + 0.15 * jax.random.normal(splits[1], (VIS,), jnp.float32), 0.25, 1.75)
    w_merge = scatter_about(splits[2], (VIS, D), VIS ** -0.5, 0.078125, ((1, 16),))
    prompt_text = scatter_about(part_splits[3], (PROMPTS * TEXT, D), 1.0, 6.0, ((0, 16),))
    norm_gain = jnp.clip(1.0 + 0.15 * jax.random.normal(splits[4], (D,), jnp.float32), 0.25, 1.75)
    w_kv = scatter_about(splits[5], (D, 2 * KVH * HD), D ** -0.5, 0.0625, ((0, 16),))
    new_query = draw_new_query(jax.random.fold_in(jax.random.fold_in(splits[15], part), 71), part)
    new_kv = draw_new_kv(jax.random.fold_in(jax.random.fold_in(splits[15], part), 71), part)
    text_len = draw_text_len(jax.random.fold_in(jax.random.fold_in(splits[15], part), 71), part)
    img_count = draw_img_count(jax.random.fold_in(jax.random.fold_in(splits[15], part), 71), part)
    img_dest_keys = jax.random.split(jax.random.fold_in(part_splits[10], 1), IMAGES // IMAGES)
    img_dest_turns = jax.random.permutation(jax.random.fold_in(part_splits[10], 3), IMAGES // IMAGES)
    img_dest = jax.vmap(lambda own, number: routed_block(jax.random.fold_in(part_splits[10], 2), own, number, IMAGES, PROMPTS, 1, IMGCAP, 1))(img_dest_keys, img_dest_turns).reshape((IMAGES, 1))
    block_dest_keys = jax.random.split(jax.random.fold_in(part_splits[11], 1), (PROMPTS * NB) // NB)
    block_dest_turns = jax.random.permutation(jax.random.fold_in(part_splits[11], 3), (PROMPTS * NB) // NB)
    block_dest = jax.vmap(lambda own, number: routed_block(jax.random.fold_in(part_splits[11], 2), own, number, NB, N_ROLE, 1, CAPB, 1))(block_dest_keys, block_dest_turns).reshape((PROMPTS * NB, 1))
    past_cache = scatter_about(part_splits[12], (N_ROLE * PASTP, BLK, 2 * KVH * HD), 1.0, 6.0, ((0, 16),))
    past_scale = jnp.clip(jnp.exp(math.log(2.0) - 1.3862944 * jax.random.uniform(part_splits[13], (N_ROLE * PASTP, 2 * KVH), jnp.float32) ** shard_levels(part_splits[13], (N_ROLE * PASTP, 2 * KVH), ((0, 16),), -0.2, 0.2)), 0.5, 2.0).astype(jnp.bfloat16)
    past_owner_keys = jax.random.split(jax.random.fold_in(part_splits[14], 1), (N_ROLE * PASTP) // PASTP)
    past_owner_turns = jax.random.permutation(jax.random.fold_in(part_splits[14], 3), (N_ROLE * PASTP) // PASTP)
    past_owner = jax.vmap(lambda own, number: routed_block(jax.random.fold_in(part_splits[14], 2), own, number, PASTP, PROMPTS, 1, max(2, 2 * PASTP // N_ROLE), 1))(past_owner_keys, past_owner_turns).reshape((N_ROLE * PASTP, 1))
    return {"images": images, "vis_gain": vis_gain, "w_merge": w_merge, "prompt_text": prompt_text, "norm_gain": norm_gain, "w_kv": w_kv, "new_query": new_query, "new_kv": new_kv, "text_len": text_len, "img_count": img_count, "img_dest": img_dest, "block_dest": block_dest, "past_cache": past_cache, "past_scale": past_scale, "past_owner": past_owner}


def normalize(values, gain_vec):
    values = values.astype(jnp.float32)
    return values * lax.rsqrt(lax.optimization_barrier(jnp.mean(values * values, axis=-1, keepdims=True)) + 1e-06) * gain_vec

def rotate(key_part):
    halfway = HD // 2
    position = jnp.arange(key_part.shape[0]).astype(jnp.float32)
    inverse = jnp.exp(jnp.arange(halfway).astype(jnp.float32) * (-2.0 * math.log(1000000.0) / HD))
    angles = position[:, None] * inverse[None, :]
    cosine = jnp.cos(angles)[:, None, :]
    sine_part = jnp.sin(angles)[:, None, :]
    front_half = key_part[..., :halfway]
    back_half = key_part[..., halfway:]
    return jnp.concatenate([front_half * cosine - back_half * sine_part, back_half * cosine + front_half * sine_part], axis=-1)

def quantize(projected):
    length = projected.shape[0]
    key_part = rotate(projected[:, :KVH * HD].reshape(length, KVH, HD))
    value_part = projected[:, KVH * HD:].reshape(length, KVH, HD)
    stacked = jnp.stack([key_part, value_part], axis=1).reshape(length // BLK, BLK, 2, KVH, HD)
    largest = lax.optimization_barrier(jnp.max(jnp.abs(stacked), axis=(1, 4)))
    scales = ((largest + 1e-05) / 448.0).astype(jnp.bfloat16)
    quantized = (stacked / scales.astype(jnp.float32)[:, None, :, :, None]).astype(jnp.bfloat16)
    return (quantized.reshape(length // BLK, BLK, 2 * KVH * HD), scales.reshape(length // BLK, 2 * KVH))

def reference(images, vis_gain, w_merge, prompt_text, norm_gain, w_kv, new_query, new_kv, text_len, img_count, img_dest, block_dest, past_cache, past_scale, past_owner):
    normed_img = normalize(images, vis_gain).astype(jnp.bfloat16)
    merged = jnp.dot(normed_img, w_merge, preferred_element_type=jnp.float32).astype(jnp.bfloat16)
    merged = merged.reshape(IMAGES, IMG_TOK, D)
    target = img_dest[:, 0]
    chosen = (target[:, None] == jnp.arange(PROMPTS)[None, :]).astype(jnp.int32)
    before = lax.optimization_barrier(jnp.sum((jnp.cumsum(chosen, axis=0) - chosen) * chosen, axis=1))
    slot_of = (target * IMGCAP + before).astype(jnp.int32)
    slot_rows = jnp.zeros((PROMPTS * IMGCAP, IMG_TOK, D), jnp.bfloat16).at[slot_of].set(merged)
    slot_count = jnp.zeros((PROMPTS * IMGCAP,), jnp.int32).at[slot_of].set(img_count)
    slot_rows = slot_rows.reshape(PROMPTS, IMGCAP * IMG_TOK, D)
    image_valid = (jnp.arange(IMG_TOK)[None, :] < slot_count[:, None]).reshape(PROMPTS, IMGCAP * IMG_TOK)
    text_valid = jnp.arange(TEXT)[None, :] < text_len[:, None]
    key_valid = jnp.concatenate([image_valid, text_valid], axis=1).reshape(PROMPTS, NB, BLK)
    text_rows = prompt_text.reshape(PROMPTS, TEXT, D)

    def prefill(inputs):
        image_part, text_part = inputs
        sequence = jnp.concatenate([image_part, text_part], axis=0)
        normed = normalize(sequence, norm_gain).astype(jnp.bfloat16)
        projected = jnp.dot(normed, w_kv, preferred_element_type=jnp.float32)
        return quantize(projected)
    quantized, scales = lax.map(prefill, (slot_rows, text_rows))
    block_target = block_dest[:, 0].reshape(PROMPTS, NB)
    chosen_block = (block_target[:, :, None] == jnp.arange(N_ROLE)[None, None, :]).astype(jnp.int32)
    before_block = lax.optimization_barrier(jnp.sum((jnp.cumsum(chosen_block, axis=1) - chosen_block) * chosen_block, axis=2))
    page_of = (block_target * PAGES + jnp.arange(PROMPTS)[:, None] * CAPB + before_block).reshape(-1).astype(jnp.int32)
    kv_cache = jnp.zeros((N_ROLE * PAGES, BLK, 2 * KVH * HD), jnp.bfloat16).at[page_of].set(quantized.reshape(PROMPTS * NB, BLK, 2 * KVH * HD))
    cache_scale = jnp.zeros((N_ROLE * PAGES, 2 * KVH), jnp.bfloat16).at[page_of].set(scales.reshape(PROMPTS * NB, 2 * KVH))
    factor = 1.0 / math.sqrt(HD)
    highest_prec = lax.Precision.HIGHEST
    page_total = N_ROLE * PASTP
    past = past_cache.astype(jnp.float32).reshape(page_total, BLK, 2, KVH, HD) * past_scale.astype(jnp.float32).reshape(page_total, 1, 2, KVH, 1)
    owners = past_owner[:, 0]

    def decode(inputs):
        quant_one, scale_one, valid_one, query_one, fresh_kv, request = inputs
        stacked = quant_one.astype(jnp.float32).reshape(NB, BLK, 2, KVH, HD) * scale_one.astype(jnp.float32).reshape(NB, 1, 2, KVH, 1)
        grouped = query_one.astype(jnp.float32).reshape(KVH, H // KVH, HD)
        scores = jnp.einsum('nbkd,kgd->kgnb', stacked[:, :, 0], grouped, precision=highest_prec) * factor
        scores = jnp.where(valid_one[None, None], scores, -1e+30)
        owned = (owners == request)[None, None, :, None]
        past_scores = jnp.einsum('nbkd,kgd->kgnb', past[:, :, 0], grouped, precision=highest_prec) * factor
        past_scores = jnp.where(owned, past_scores, -1e+30)
        fresh_vals = fresh_kv.astype(jnp.float32).reshape(2, KVH, HD)
        own_score = jnp.einsum('kd,kgd->kg', fresh_vals[0], grouped, precision=highest_prec) * factor
        highest = jnp.maximum(jnp.maximum(lax.optimization_barrier(jnp.max(scores, axis=(2, 3))), lax.optimization_barrier(jnp.max(past_scores, axis=(2, 3)))), own_score)
        weights = jnp.where(valid_one[None, None], jnp.exp(scores - highest[:, :, None, None]), 0.0)
        past_weights = jnp.where(owned, jnp.exp(past_scores - highest[:, :, None, None]), 0.0)
        own_weight = jnp.exp(own_score - highest)
        total_sum = lax.optimization_barrier(jnp.sum(weights, axis=(2, 3))) + lax.optimization_barrier(jnp.sum(past_weights, axis=(2, 3))) + own_weight
        summed = jnp.einsum('kgnb,nbkd->kgd', weights, stacked[:, :, 1], precision=highest_prec)
        summed = summed + jnp.einsum('kgnb,nbkd->kgd', past_weights, past[:, :, 1], precision=highest_prec)
        summed = summed + own_weight[:, :, None] * fresh_vals[1][:, None, :]
        return (summed / total_sum[:, :, None]).reshape(H * HD).astype(jnp.bfloat16)
    requests = jnp.arange(PROMPTS).astype(jnp.int32)
    attended = lax.map(decode, (quantized, scales, key_valid, new_query, new_kv, requests))
    return (kv_cache, cache_scale, attended)
```

```python
import functools
import math

import jax
import jax.numpy as jnp
from jax import lax
from jax.experimental import pallas as pl
from jax.experimental.pallas import tpu as pltpu
from jax.sharding import PartitionSpec as P

H = 64
KVH = 8
HD = 128
IMG_TOK = 8
IMGCAP = 4
BLK = 16


MESH = pl.DeviceIdType.MESH
CHUNK = 512


def normalize(values, gain_vec):
    values = values.astype(jnp.float32)
    return values * lax.rsqrt(jnp.mean(values * values, axis=-1, keepdims=True) + 1e-06) * gain_vec


def rotate(key_part):
    halfway = HD // 2
    position = jnp.arange(key_part.shape[0]).astype(jnp.float32)
    inverse = jnp.exp(jnp.arange(halfway).astype(jnp.float32) * (-2.0 * math.log(1000000.0) / HD))
    angles = position[:, None] * inverse[None, :]
    cosine = jnp.cos(angles)[:, None, :]
    sine_part = jnp.sin(angles)[:, None, :]
    front_half = key_part[..., :halfway]
    back_half = key_part[..., halfway:]
    return jnp.concatenate(
        [front_half * cosine - back_half * sine_part, back_half * cosine + front_half * sine_part],
        axis=-1,
    )


def quantize(projected):
    length = projected.shape[0]
    key_part = rotate(projected[:, : KVH * HD].reshape(length, KVH, HD))
    value_part = projected[:, KVH * HD :].reshape(length, KVH, HD)
    stacked = jnp.stack([key_part, value_part], axis=1).reshape(length // BLK, BLK, 2, KVH, HD)
    largest = jnp.max(jnp.abs(stacked), axis=(1, 4))
    scales = ((largest + 1e-05) / 448.0).astype(jnp.bfloat16)
    quantized = (stacked / scales.astype(jnp.float32)[:, None, :, :, None]).astype(jnp.bfloat16)
    return (
        quantized.reshape(length // BLK, BLK, 2 * KVH * HD),
        scales.reshape(length // BLK, 2 * KVH),
    )


def combine(earlier, later):
    left_top, left_total, left_summed = earlier
    right_top, right_total, right_summed = later
    highest = jnp.maximum(left_top, right_top)
    left_factor = jnp.exp(left_top - highest)
    right_factor = jnp.exp(right_top - highest)
    return (
        highest,
        left_total * left_factor + right_total * right_factor,
        left_summed * left_factor[..., None] + right_summed * right_factor[..., None],
    )


def front_kernel(
    n, payload, vis_gain, w_merge, text, norm_gain, w_kv,
    projected, extras,
    ibuf, wm, nimg, mout, mbuf, abuf, arecv, wq, csend, crecv,
    img_s, img_r, sib_s, sib_r, mrg_s, mrg_r, at_s, at_r, ai_s, ai_r,
    z_s, z_r, ws_s, ws_r, c_s, c_r, loc,
):
    nz = n // 4
    chips = n // 2
    vis = vis_gain.shape[1]
    x = lax.axis_index("outer")
    r = lax.axis_index("role")
    z = r // 4
    y = (r // 2) % 2
    c = r % 2
    q = r // 2
    sib = q * 2 + (1 - c)
    width = w_merge.shape[1]
    half = width // 2
    rows_t = text.shape[0]
    rows_i = IMGCAP * IMG_TOK
    mine = y * 2 + x

    def rdma(src, dst, ss, rs, outer, role):
        return pltpu.make_async_remote_copy(
            src_ref=src, dst_ref=dst, send_sem=ss, recv_sem=rs,
            device_id=(outer, role), device_id_type=MESH,
        )

    def member(d):
        dx, dy = d % 2, d // 2
        ox, oy = (x + dx) % 2, (y + dy) % 2
        return oy * 2 + ox, ox, z * 4 + oy * 2 + c

    barrier = pltpu.get_barrier_semaphore()
    for k in range(1, n):
        pl.semaphore_signal(barrier, inc=1, device_id=(x, (r + k) % n), device_id_type=MESH)
    for d in (1, 3):
        _, ox, role = member(d)
        pl.semaphore_signal(barrier, inc=1, device_id=(ox, role), device_id_type=MESH)
    wm_copy = pltpu.make_async_copy(w_merge, wm, loc.at[0])
    wm_copy.start()
    pl.semaphore_wait(barrier, n + 1)

    def img_copy(k):
        slot = ibuf.at[r]
        return rdma(payload, slot, img_s.at[k], img_r.at[k], x, ((q + k) % chips) * 2 + c)

    for k in range(1, chips):
        img_copy(k).start()
    rdma(payload, ibuf.at[r], sib_s.at[0], sib_r.at[0], x, sib).start()
    own_img = pltpu.make_async_copy(payload, ibuf.at[r], loc.at[1])
    own_img.start()

    def piece(zz, core):
        return wq.at[pl.ds(pl.multiple_of((zz * 2 + core) * half, half), half), :]

    own_rows = w_kv.at[pl.ds(pl.multiple_of(x * half, half), half), :]
    own_w = pltpu.make_async_copy(own_rows, piece(z, c), loc.at[2])
    own_w.start()

    def z_copy(way, t, src, zz):
        role = ((z + (1 if way == 0 else nz - 1)) % nz) * 4 + y * 2 + c
        return rdma(src, piece(zz, c), z_s.at[way, t], z_r.at[way, t], x, role)

    def w_sib(i, src, zz):
        return rdma(src, piece(zz, c), ws_s.at[i], ws_r.at[i], x, sib)

    @pl.when(z < nz - 1)
    def _():
        z_copy(0, 1, own_rows, z).start()

    @pl.when(z > 0)
    def _():
        z_copy(1, 1, own_rows, z).start()

    w_sib(0, own_rows, z).start()

    def norm_rows(i, carry):
        at = pl.multiple_of(i * 16, 16)
        v = text[pl.ds(at, 16), :].astype(jnp.float32)
        inv = lax.rsqrt(jnp.mean(v * v, axis=1, keepdims=True) + 1e-06)
        v = (v * inv * norm_gain[...]).astype(jnp.bfloat16)
        for g in range(4):
            for s in range(chips):
                col = (s // 2) * 4 * width + (g // 2) * 2 * width + (s % 2) * width + (g % 2) * half
                abuf[g, pl.ds(rows_i + at, 16), s * half : (s + 1) * half] = v[:, col : col + half]
        return carry

    lax.fori_loop(0, rows_t // 16, norm_rows, 0)

    def a_copy(d, lo, size, ss, rs):
        g, ox, role = member(d)
        return rdma(
            abuf.at[g, pl.ds(lo, size), :], arecv.at[d - 1, pl.ds(lo, size), :],
            ss.at[d - 1], rs.at[d - 1], ox, role,
        )

    for d in range(1, 4):
        a_copy(d, rows_i, rows_t, at_s, at_r).start()

    own_img.wait()
    for k in range(1, chips):
        src = ((q + chips - k) % chips) * 2 + c
        rdma(payload, ibuf.at[src], img_s.at[k], img_r.at[k], x, sib).wait_recv()
        rdma(ibuf.at[src], ibuf.at[src], sib_s.at[k], sib_r.at[k], x, sib).start()
    for k in range(chips):
        src = ((q + chips - k) % chips) * 2 + (1 - c)
        rdma(payload, ibuf.at[src], sib_s.at[k], sib_r.at[k], x, sib).wait_recv()

    def norm_images(i, carry):
        v = ibuf[i, :, :vis].astype(jnp.float32)
        inv = lax.rsqrt(jnp.mean(v * v, axis=1, keepdims=True) + 1e-06)
        nimg[pl.ds(pl.multiple_of(i * 16, 16), 16), :] = (v * inv * vis_gain[...]).astype(jnp.bfloat16)
        extras[i, :, :] = ibuf[i, :, vis:]
        return carry

    lax.fori_loop(0, n, norm_images, 0)
    wm_copy.wait()
    merged = jnp.dot(nimg[...], wm[...], preferred_element_type=jnp.float32).astype(jnp.bfloat16)

    images = 2 * n
    lane = lax.broadcasted_iota(jnp.int32, (1, images * IMG_TOK), 1)
    image = lane // IMG_TOK
    last = ibuf.shape[2]
    named = [
        jnp.concatenate(
            [ibuf[i // 2, i % 2 : i % 2 + 1, last - 128 :].astype(jnp.float32)] * (images * IMG_TOK // 128), axis=1
        )
        for i in range(images)
    ]
    target = jnp.zeros(lane.shape, jnp.float32)
    for i in range(images):
        target = jnp.where(image == i, named[i], target)
    place = target * float(IMGCAP)
    for i in range(images):
        place = place + jnp.where((image > i) & (named[i] == target), 1.0, 0.0)
    row = lax.broadcasted_iota(jnp.int32, (n * rows_i, images * IMG_TOK), 0)
    col = lax.broadcasted_iota(jnp.int32, (n * rows_i, images * IMG_TOK), 1)
    hot = ((row // IMG_TOK).astype(jnp.float32) == place) & (row % IMG_TOK == col % IMG_TOK)
    placed = jnp.dot(
        jnp.where(hot, 1.0, 0.0).astype(jnp.bfloat16), merged, preferred_element_type=jnp.float32
    ).astype(jnp.bfloat16)
    for p in range(n):
        mout[p] = placed[p * rows_i : (p + 1) * rows_i]
    for k in range(1, n):
        to = (r + k) % n
        rdma(mout.at[to], mbuf.at[r], mrg_s.at[k], mrg_r.at[k], x, to).start()
    own_m = pltpu.make_async_copy(mout.at[r], mbuf.at[r], loc.at[1])
    own_m.start()
    own_m.wait()

    def hop(t):
        @pl.when(z - t >= 0)
        def _():
            z_copy(0, t, own_rows, z - t).wait_recv()

            @pl.when(z < nz - 1)
            def _():
                z_copy(0, t + 1, piece(z - t, c), z - t).start()

            w_sib(t, piece(z - t, c), z - t).start()

        @pl.when(z + t < nz)
        def _():
            z_copy(1, t, own_rows, z + t).wait_recv()

            @pl.when(z > 0)
            def _():
                z_copy(1, t + 1, piece(z + t, c), z + t).start()

            w_sib(nz - 1 + t, piece(z + t, c), z + t).start()

    hop(1)
    for k in range(1, n):
        src = (r + n - k) % n
        rdma(mout.at[src], mbuf.at[src], mrg_s.at[k], mrg_r.at[k], x, sib).wait_recv()
    squares = jnp.zeros((rows_i, 1), jnp.float32)
    for s in range(n):
        v = mbuf[s].astype(jnp.float32)
        squares = squares + jnp.sum(v * v, axis=1, keepdims=True)
    inv = lax.rsqrt(squares / float(n * width) + 1e-06)
    for s in range(n):
        v = (mbuf[s].astype(jnp.float32) * inv * norm_gain[:, s * width : (s + 1) * width]).astype(jnp.bfloat16)
        spot = (s // 4) * 2 + s % 2
        for e in range(2):
            abuf[((s // 2) % 2) * 2 + e, 0:rows_i, spot * half : (spot + 1) * half] = v[:, e * half : (e + 1) * half]
    for d in range(1, 4):
        a_copy(d, 0, rows_i, ai_s, ai_r).start()

    for t in range(2, nz):
        hop(t)
    own_w.wait()
    w_sib(0, own_rows, z).wait_recv()
    for t in range(1, nz):
        @pl.when(z - t >= 0)
        def _():
            w_sib(t, own_rows, z - t).wait_recv()

        @pl.when(z + t < nz)
        def _():
            w_sib(nz - 1 + t, own_rows, z + t).wait_recv()

    kv_width = w_kv.shape[1]
    for d in range(1, 4):
        a_copy(d, rows_i, rows_t, at_s, at_r).wait()
        a_copy(d, 0, rows_i, ai_s, ai_r).wait()

    def c_copy(d, j):
        _, ox, role = member(d)
        return rdma(csend.at[d - 1, j], crecv.at[d - 1, j], c_s.at[d - 1, j], c_r.at[d - 1, j], ox, role)

    parts = kv_width // CHUNK

    def partials(j, carry):
        cols = pl.ds(pl.multiple_of(j * CHUNK, CHUNK), CHUNK)
        for d in (3, 1, 2):
            csend[d - 1, j] = jnp.dot(
                arecv[d - 1], wq[:, cols], preferred_element_type=jnp.float32
            ).astype(jnp.bfloat16)
            c_copy(d, j).start()
        return carry

    lax.fori_loop(0, parts, partials, 0)

    def own_partial(j, carry):
        cols = pl.ds(pl.multiple_of(j * CHUNK, CHUNK), CHUNK)
        projected[:, cols] = jnp.dot(abuf[mine], wq[:, cols], preferred_element_type=jnp.float32)
        return carry

    lax.fori_loop(0, parts, own_partial, 0)

    def add_partials(j, carry):
        cols = pl.ds(pl.multiple_of(j * CHUNK, CHUNK), CHUNK)
        for d in range(1, 4):
            c_copy(d, j).wait()
        projected[:, cols] = (
            projected[:, cols]
            + crecv[0, j].astype(jnp.float32)
            + crecv[1, j].astype(jnp.float32)
            + crecv[2, j].astype(jnp.float32)
        )
        return carry

    lax.fori_loop(0, parts, add_partials, 0)

    for k in range(1, chips):
        img_copy(k).wait_send()
    for k in range(chips):
        rdma(payload, ibuf.at[r], sib_s.at[k], sib_r.at[k], x, sib).wait_send()
    for k in range(1, n):
        rdma(mout.at[r], mbuf.at[r], mrg_s.at[k], mrg_r.at[k], x, sib).wait_send()
    w_sib(0, own_rows, z).wait_send()
    for t in range(1, nz):
        @pl.when((z - t + 1 >= 0) & (z < nz - 1))
        def _():
            z_copy(0, t, own_rows, z).wait_send()

        @pl.when((z + t - 1 < nz) & (z > 0))
        def _():
            z_copy(1, t, own_rows, z).wait_send()

        @pl.when(z - t >= 0)
        def _():
            w_sib(t, own_rows, z).wait_send()

        @pl.when(z + t < nz)
        def _():
            w_sib(nz - 1 + t, own_rows, z).wait_send()


def front(payload, vis_gain, w_merge, text, norm_gain, w_kv):
    n = lax.axis_size("role")
    nz = n // 4
    chips = n // 2
    width = w_merge.shape[1]
    vis = vis_gain.shape[0]
    model = norm_gain.shape[0]
    rows_i = IMGCAP * IMG_TOK
    length = text.shape[0] + rows_i
    kv_width = w_kv.shape[1]
    parts = kv_width // CHUNK
    bf = jnp.bfloat16
    dma = pltpu.SemaphoreType.DMA
    vmem = pl.BlockSpec(memory_space=pltpu.VMEM)
    hbm = pl.BlockSpec(memory_space=pl.ANY)
    return pl.pallas_call(
        functools.partial(front_kernel, n),
        out_shape=(
            jax.ShapeDtypeStruct((length, kv_width), jnp.float32),
            jax.ShapeDtypeStruct((n, 16, payload.shape[1] - vis), bf),
        ),
        in_specs=[hbm, vmem, hbm, vmem, vmem, hbm],
        out_specs=(vmem, vmem),
        scratch_shapes=[
            pltpu.VMEM((n,) + payload.shape, bf),
            pltpu.VMEM(w_merge.shape, bf),
            pltpu.VMEM((n * 16, vis), bf),
            pltpu.VMEM((n, rows_i, width), bf),
            pltpu.VMEM((n, rows_i, width), bf),
            pltpu.VMEM((4, length, model // 4), bf),
            pltpu.VMEM((3, length, model // 4), bf),
            pltpu.VMEM((model // 4, kv_width), bf),
            pltpu.VMEM((3, parts, length, CHUNK), bf),
            pltpu.VMEM((3, parts, length, CHUNK), bf),
            dma((chips,)), dma((chips,)), dma((chips,)), dma((chips,)),
            dma((n,)), dma((n,)), dma((3,)), dma((3,)), dma((3,)), dma((3,)),
            dma((2, nz + 1)), dma((2, nz + 1)), dma((2 * nz,)), dma((2 * nz,)),
            dma((3, parts)), dma((3, parts)), dma((3,)),
        ],
        compiler_params=pltpu.CompilerParams(
            collective_id=0, has_side_effects=True, vmem_limit_bytes=56 * 1024 * 1024
        ),
        name="front",
    )(payload, vis_gain[None, :], w_merge, text, norm_gain[None, :], w_kv)


def tail(
    projected, every_query, counts, targets,
    new_query, new_kv, text_len, block_dest, past_cache, past_scale, past_owner,
):
    rank_count = lax.axis_size("role")
    myself = lax.axis_index("role")
    groups = H // KVH
    factor = 1.0 / math.sqrt(HD)
    highest_prec = lax.Precision.HIGHEST
    bf = jnp.bfloat16
    length, kv_width = projected.shape
    chosen = (targets[:, None] == jnp.arange(rank_count)[None, :]).astype(jnp.int32)
    before = jnp.sum((jnp.cumsum(chosen, axis=0) - chosen) * chosen, axis=1)
    slot_of = targets * IMGCAP + before
    is_mine = slot_of[None, :] == myself * IMGCAP + jnp.arange(IMGCAP)[:, None]
    slot_count = jnp.sum(jnp.where(is_mine, counts[None, :], 0), axis=1)
    image_valid = (jnp.arange(IMG_TOK)[None, :] < slot_count[:, None]).reshape(-1)
    text_valid = jnp.arange(length - IMGCAP * IMG_TOK) < text_len[0]
    key_valid = jnp.concatenate([image_valid, text_valid])
    quantized, scales = quantize(projected)
    blocks = length // BLK
    per_rank = blocks // rank_count + 1
    block_target = block_dest[:, 0]
    chosen_block = (block_target[:, None] == jnp.arange(rank_count)[None, :]).astype(jnp.int32)
    before_block = jnp.sum((jnp.cumsum(chosen_block, axis=0) - chosen_block) * chosen_block, axis=1)
    page_of = block_target * per_rank + before_block
    routing = (page_of[None, :] == jnp.arange(rank_count * per_rank)[:, None]).astype(bf)
    send_quant = jnp.dot(
        routing, quantized.reshape(blocks, BLK * kv_width), preferred_element_type=jnp.float32
    )
    send_quant = send_quant.astype(bf).reshape(rank_count, per_rank, BLK, kv_width)
    small = jnp.concatenate([scales, key_valid.reshape(blocks, BLK).astype(bf)], axis=1)
    send_small = (
        jnp.dot(routing, small, preferred_element_type=jnp.float32)
        .astype(bf)
        .reshape(rank_count, per_rank, 2 * KVH + BLK)
    )
    kv_cache, got_small = (
        lax.all_to_all(send_quant, "role", split_axis=0, concat_axis=0, tiled=True),
        lax.all_to_all(send_small, "role", split_axis=0, concat_axis=0, tiled=True),
    )
    cache_scale, cache_valid = got_small[..., : 2 * KVH], got_small[..., 2 * KVH :]
    query = every_query.reshape(rank_count, KVH, groups, HD)

    past_pages = past_cache.shape[0]
    owner_hot = past_owner[:, 0][:, None] == jnp.arange(rank_count)[None, :]
    past_stack = past_cache.reshape(past_pages, BLK, 2, KVH, HD)
    past_factor = past_scale.astype(jnp.float32).reshape(past_pages, 2, KVH)[..., None, None]
    page_query = jnp.dot(
        owner_hot.astype(bf), every_query, preferred_element_type=jnp.float32
    ).astype(bf).reshape(past_pages, KVH, groups, HD)
    page_scores = (
        jnp.einsum("pbkd,pkgd->pkgb", past_stack[:, :, 0], page_query, preferred_element_type=jnp.float32)
        * past_factor[:, 0]
        * factor
    )
    page_top = jnp.max(page_scores, axis=3)
    page_weights = jnp.exp(page_scores - page_top[..., None])
    page_sum_w = jnp.sum(page_weights, axis=3)
    page_summed = jnp.einsum(
        "pkgb,pbkd->pkgd", (page_weights * past_factor[:, 1]).astype(bf), past_stack[:, :, 1],
        preferred_element_type=jnp.float32,
    )
    owned_mask = owner_hot[:, :, None, None]
    masked_top = jnp.where(owned_mask, page_top[:, None], -1e30)
    past_top = jnp.max(masked_top, axis=0)
    page_factor = jnp.where(owned_mask, jnp.exp(masked_top - past_top[None]), 0.0)
    past_total = jnp.sum(page_factor * page_sum_w[:, None], axis=0)
    past_summed = jnp.einsum("prkg,pkgd->rkgd", page_factor, page_summed, precision=highest_prec)

    stacked = kv_cache.reshape(rank_count, per_rank, BLK, 2, KVH, HD)
    in_factor = cache_scale.astype(jnp.float32).reshape(rank_count, per_rank, 2, KVH)
    key_factor = jnp.transpose(in_factor[:, :, 0], (0, 2, 1))[:, :, None, :, None]
    value_factor = jnp.transpose(in_factor[:, :, 1], (0, 2, 1))[:, :, None, :, None]
    scores = (
        jnp.einsum("scbkd,skgd->skgcb", stacked[:, :, :, 0], query, preferred_element_type=jnp.float32)
        * key_factor
        * factor
    )
    present = cache_valid.astype(jnp.float32)[:, None, None] > 0.5
    scores = jnp.where(present, scores, -1e30)
    highest = jnp.max(scores, axis=(3, 4))
    weights = jnp.where(present, jnp.exp(scores - highest[..., None, None]), 0.0)
    total_sum = jnp.sum(weights, axis=(3, 4))
    summed = jnp.einsum(
        "skgcb,scbkd->skgd", (weights * value_factor).astype(bf), stacked[:, :, :, 1],
        preferred_element_type=jnp.float32,
    )
    highest, total_sum, summed = combine(
        (highest, total_sum, summed), (past_top, past_total, past_summed)
    )
    packed = jnp.concatenate(
        [
            summed.reshape(rank_count, H, HD),
            jnp.concatenate(
                [highest.reshape(rank_count, 1, H), total_sum.reshape(rank_count, 1, H)], axis=2
            ),
        ],
        axis=1,
    )
    got = lax.all_to_all(packed, "role", split_axis=0, concat_axis=0, tiled=True)
    tops, totals, sums = got[:, H, :H], got[:, H, H : 2 * H], got[:, :H]
    fresh_vals = new_kv[0].astype(jnp.float32).reshape(2, KVH, HD)
    own_query = new_query[0].astype(jnp.float32).reshape(KVH, groups, HD)
    own_score = (jnp.sum(fresh_vals[0][:, None] * own_query, axis=2) * factor).reshape(H)
    final_top = jnp.maximum(jnp.max(tops, axis=0), own_score)
    old_factor = jnp.exp(tops - final_top)
    own_weight = jnp.exp(own_score - final_top)
    final_total = jnp.sum(totals * old_factor, axis=0) + own_weight
    own_value = jnp.repeat(fresh_vals[1], groups, axis=0)
    final_summed = jnp.sum(sums * old_factor[..., None], axis=0) + own_weight[:, None] * own_value
    attended = (final_summed / final_total[:, None]).reshape(1, H * HD).astype(bf)
    return (
        kv_cache.reshape(rank_count * per_rank, BLK, kv_width),
        cache_scale.reshape(rank_count * per_rank, 2 * KVH),
        attended,
    )


def plain_front(images, vis_gain, w_merge, prompt_text, norm_gain, w_kv, targets):
    rank_count = lax.axis_size("role")
    columns = w_merge.shape[1]
    normed_img = normalize(lax.all_gather(images, "role", axis=0, tiled=True), vis_gain).astype(
        jnp.bfloat16
    )
    merged = jnp.dot(normed_img, w_merge, preferred_element_type=jnp.float32).astype(jnp.bfloat16)
    image_total = targets.shape[0]
    chosen = (targets[:, None] == jnp.arange(rank_count)[None, :]).astype(jnp.int32)
    before = jnp.sum((jnp.cumsum(chosen, axis=0) - chosen) * chosen, axis=1)
    slot_of = targets * IMGCAP + before
    placing = (slot_of[None, :] == jnp.arange(rank_count * IMGCAP)[:, None]).astype(jnp.bfloat16)
    outgoing = jnp.dot(
        placing, merged.reshape(image_total, IMG_TOK * columns), preferred_element_type=jnp.float32
    )
    outgoing = outgoing.astype(jnp.bfloat16).reshape(rank_count, IMGCAP * IMG_TOK, columns)
    arrived = lax.all_to_all(outgoing, "role", split_axis=0, concat_axis=2, tiled=True)
    image_part = arrived.reshape(IMGCAP * IMG_TOK, rank_count * columns)
    sequence = jnp.concatenate([image_part, prompt_text], axis=0)
    normed = normalize(sequence, norm_gain).astype(jnp.bfloat16)
    rows = lax.all_gather(w_kv, "role", axis=0, tiled=True)
    return jnp.dot(normed, rows, preferred_element_type=jnp.float32)


def body(
    paired,
    images,
    vis_gain,
    w_merge,
    prompt_text,
    norm_gain,
    w_kv,
    new_query,
    new_kv,
    text_len,
    img_count,
    img_dest,
    block_dest,
    past_cache,
    past_scale,
    past_owner,
):
    n = lax.axis_size("role")
    if paired and images.shape[0] == 2 * IMG_TOK:
        meta = jnp.concatenate([img_dest[:, 0], img_count]).astype(jnp.bfloat16)
        meta = jnp.pad(meta, (0, 12))[:, None] * jnp.ones((1, 128), jnp.bfloat16)
        payload = jnp.concatenate([images, new_query.reshape(16, -1), meta], axis=1)
        projected, extras = front(payload, vis_gain, w_merge, prompt_text, norm_gain, w_kv)
        every_query = extras[:, :, :-128].reshape(n, -1)
        numbers = extras[:, :4, -1].astype(jnp.int32)
        targets = numbers[:, :2].reshape(-1)
        counts = numbers[:, 2:].reshape(-1)
    else:
        counts, targets = (
            lax.all_gather(img_count, "role", axis=0, tiled=True),
            lax.all_gather(img_dest[:, 0], "role", axis=0, tiled=True),
        )
        every_query = lax.all_gather(new_query, "role", axis=0, tiled=True)
        projected = plain_front(images, vis_gain, w_merge, prompt_text, norm_gain, w_kv, targets)
    return tail(
        projected, every_query, counts, targets,
        new_query, new_kv, text_len, block_dest, past_cache, past_scale, past_owner,
    )


def solution(mesh):
    in_specs = (
        P(("outer", "role"), None),
        P(),
        P(None, "role"),
        P(("outer", "role"), None),
        P(),
        P("role", None),
        P(("outer", "role"), None),
        P(("outer", "role"), None),
        P(("outer", "role")),
        P(("outer", "role")),
        P(("outer", "role"), None),
        P(("outer", "role"), None),
        P(("outer", "role"), None, None),
        P(("outer", "role"), None),
        P(("outer", "role"), None),
    )
    out_specs = (
        P(("outer", "role"), None, None),
        P(("outer", "role"), None),
        P(("outer", "role"), None),
    )
    paired = mesh.shape["outer"] == 2 and mesh.shape["role"] % 8 == 0
    return jax.shard_map(
        functools.partial(body, paired), mesh=mesh, in_specs=in_specs, out_specs=out_specs, check_vma=False
    )
```

```python
import functools
import math

import jax
import jax.numpy as jnp
from jax import lax
from jax.experimental import pallas as pl
from jax.experimental.pallas import tpu as pltpu
from jax.sharding import PartitionSpec as P

H = 64
KVH = 8
HD = 128
IMG_TOK = 8
IMGCAP = 4
BLK = 16


MESH = pl.DeviceIdType.MESH
CHUNK = 512


def normalize(values, gain_vec):
    values = values.astype(jnp.float32)
    return values * lax.rsqrt(jnp.mean(values * values, axis=-1, keepdims=True) + 1e-06) * gain_vec


def rotate(key_part):
    halfway = HD // 2
    position = jnp.arange(key_part.shape[0]).astype(jnp.float32)
    inverse = jnp.exp(jnp.arange(halfway).astype(jnp.float32) * (-2.0 * math.log(1000000.0) / HD))
    angles = position[:, None] * inverse[None, :]
    cosine = jnp.cos(angles)[:, None, :]
    sine_part = jnp.sin(angles)[:, None, :]
    front_half = key_part[..., :halfway]
    back_half = key_part[..., halfway:]
    return jnp.concatenate(
        [front_half * cosine - back_half * sine_part, back_half * cosine + front_half * sine_part],
        axis=-1,
    )


def quantize(projected):
    length = projected.shape[0]
    key_part = rotate(projected[:, : KVH * HD].reshape(length, KVH, HD))
    value_part = projected[:, KVH * HD :].reshape(length, KVH, HD)
    stacked = jnp.stack([key_part, value_part], axis=1).reshape(length // BLK, BLK, 2, KVH, HD)
    largest = jnp.max(jnp.abs(stacked), axis=(1, 4))
    scales = ((largest + 1e-05) / 448.0).astype(jnp.bfloat16)
    quantized = (stacked / scales.astype(jnp.float32)[:, None, :, :, None]).astype(jnp.bfloat16)
    return (
        quantized.reshape(length // BLK, BLK, 2 * KVH * HD),
        scales.reshape(length // BLK, 2 * KVH),
    )


def combine(earlier, later):
    left_top, left_total, left_summed = earlier
    right_top, right_total, right_summed = later
    highest = jnp.maximum(left_top, right_top)
    left_factor = jnp.exp(left_top - highest)
    right_factor = jnp.exp(right_top - highest)
    return (
        highest,
        left_total * left_factor + right_total * right_factor,
        left_summed * left_factor[..., None] + right_summed * right_factor[..., None],
    )


def front_kernel(
    n, payload, vis_gain, w_merge, text, norm_gain, w_kv,
    projected, extras,
    ibuf, wm, nimg, mout, mbuf, abuf, arecv, wq, csend, crecv,
    img_s, img_r, sib_s, sib_r, mrg_s, mrg_r, at_s, at_r, ai_s, ai_r,
    z_s, z_r, ws_s, ws_r, c_s, c_r, loc,
):
    nz = n // 4
    chips = n // 2
    vis = vis_gain.shape[1]
    x = lax.axis_index("outer")
    r = lax.axis_index("role")
    z = r // 4
    y = (r // 2) % 2
    c = r % 2
    q = r // 2
    sib = q * 2 + (1 - c)
    width = w_merge.shape[1]
    half = width // 2
    rows_t = text.shape[0]
    rows_i = IMGCAP * IMG_TOK
    mine = y * 2 + x

    def rdma(src, dst, ss, rs, outer, role):
        return pltpu.make_async_remote_copy(
            src_ref=src, dst_ref=dst, send_sem=ss, recv_sem=rs,
            device_id=(outer, role), device_id_type=MESH,
        )

    def member(d):
        dx, dy = d % 2, d // 2
        ox, oy = (x + dx) % 2, (y + dy) % 2
        return oy * 2 + ox, ox, z * 4 + oy * 2 + c

    barrier = pltpu.get_barrier_semaphore()
    for k in range(1, n):
        pl.semaphore_signal(barrier, inc=1, device_id=(x, (r + k) % n), device_id_type=MESH)
    for d in (1, 3):
        _, ox, role = member(d)
        pl.semaphore_signal(barrier, inc=1, device_id=(ox, role), device_id_type=MESH)
    wm_copy = pltpu.make_async_copy(w_merge, wm, loc.at[0])
    wm_copy.start()
    pl.semaphore_wait(barrier, n + 1)

    def img_copy(k):
        slot = ibuf.at[r]
        return rdma(payload, slot, img_s.at[k], img_r.at[k], x, ((q + k) % chips) * 2 + c)

    for k in range(1, chips):
        img_copy(k).start()
    rdma(payload, ibuf.at[r], sib_s.at[0], sib_r.at[0], x, sib).start()
    own_img = pltpu.make_async_copy(payload, ibuf.at[r], loc.at[1])
    own_img.start()

    kv_width = w_kv.shape[1]
    side = kv_width // 2

    def piece(h, zz, core):
        at = pl.multiple_of((zz * 2 + core) * half, half)
        return wq.at[pl.ds(at, half), h * side : (h + 1) * side]

    def own_rows(h):
        return w_kv.at[pl.ds(pl.multiple_of(x * half, half), half), h * side : (h + 1) * side]

    own_w = [pltpu.make_async_copy(own_rows(h), piece(h, z, c), loc.at[2 + h]) for h in range(2)]

    def z_copy(h, way, t, src, zz):
        role = ((z + (1 if way == 0 else nz - 1)) % nz) * 4 + y * 2 + c
        return rdma(src, piece(h, zz, c), z_s.at[h, way, t], z_r.at[h, way, t], x, role)

    def w_sib(h, i, src, zz):
        return rdma(src, piece(h, zz, c), ws_s.at[h, i], ws_r.at[h, i], x, sib)

    def launch(h):
        @pl.when(z < nz - 1)
        def _():
            z_copy(h, 0, 1, own_rows(h), z).start()

        @pl.when(z > 0)
        def _():
            z_copy(h, 1, 1, own_rows(h), z).start()

        own_w[h].start()
        w_sib(h, 0, own_rows(h), z).start()

    launch(0)

    def norm_rows(i, carry):
        at = pl.multiple_of(i * 16, 16)
        v = text[pl.ds(at, 16), :].astype(jnp.float32)
        inv = lax.rsqrt(jnp.mean(v * v, axis=1, keepdims=True) + 1e-06)
        v = (v * inv * norm_gain[...]).astype(jnp.bfloat16)
        for g in range(4):
            for s in range(chips):
                col = (s // 2) * 4 * width + (g // 2) * 2 * width + (s % 2) * width + (g % 2) * half
                abuf[g, pl.ds(rows_i + at, 16), s * half : (s + 1) * half] = v[:, col : col + half]
        return carry

    lax.fori_loop(0, rows_t // 16, norm_rows, 0)

    def a_copy(d, lo, size, ss, rs):
        g, ox, role = member(d)
        return rdma(
            abuf.at[g, pl.ds(lo, size), :], arecv.at[d - 1, pl.ds(lo, size), :],
            ss.at[d - 1], rs.at[d - 1], ox, role,
        )

    for d in range(1, 4):
        a_copy(d, rows_i, rows_t, at_s, at_r).start()

    own_img.wait()
    for k in range(1, chips):
        src = ((q + chips - k) % chips) * 2 + c
        rdma(payload, ibuf.at[src], img_s.at[k], img_r.at[k], x, sib).wait_recv()
        rdma(ibuf.at[src], ibuf.at[src], sib_s.at[k], sib_r.at[k], x, sib).start()
    for k in range(chips):
        src = ((q + chips - k) % chips) * 2 + (1 - c)
        rdma(payload, ibuf.at[src], sib_s.at[k], sib_r.at[k], x, sib).wait_recv()

    def norm_images(i, carry):
        v = ibuf[i, :, :vis].astype(jnp.float32)
        inv = lax.rsqrt(jnp.mean(v * v, axis=1, keepdims=True) + 1e-06)
        nimg[pl.ds(pl.multiple_of(i * 16, 16), 16), :] = (v * inv * vis_gain[...]).astype(jnp.bfloat16)
        extras[i, :, :] = ibuf[i, :, vis:]
        return carry

    lax.fori_loop(0, n, norm_images, 0)
    wm_copy.wait()
    merged = jnp.dot(nimg[...], wm[...], preferred_element_type=jnp.float32).astype(jnp.bfloat16)

    images = 2 * n
    lane = lax.broadcasted_iota(jnp.int32, (1, images * IMG_TOK), 1)
    image = lane // IMG_TOK
    last = ibuf.shape[2]
    named = [
        jnp.concatenate(
            [ibuf[i // 2, i % 2 : i % 2 + 1, last - 128 :].astype(jnp.float32)] * (images * IMG_TOK // 128), axis=1
        )
        for i in range(images)
    ]
    target = jnp.zeros(lane.shape, jnp.float32)
    for i in range(images):
        target = jnp.where(image == i, named[i], target)
    place = target * float(IMGCAP)
    for i in range(images):
        place = place + jnp.where((image > i) & (named[i] == target), 1.0, 0.0)
    row = lax.broadcasted_iota(jnp.int32, (n * rows_i, images * IMG_TOK), 0)
    col = lax.broadcasted_iota(jnp.int32, (n * rows_i, images * IMG_TOK), 1)
    hot = ((row // IMG_TOK).astype(jnp.float32) == place) & (row % IMG_TOK == col % IMG_TOK)
    placed = jnp.dot(
        jnp.where(hot, 1.0, 0.0).astype(jnp.bfloat16), merged, preferred_element_type=jnp.float32
    ).astype(jnp.bfloat16)
    for p in range(n):
        mout[p] = placed[p * rows_i : (p + 1) * rows_i]
    for k in range(1, n):
        to = (r + k) % n
        rdma(mout.at[to], mbuf.at[r], mrg_s.at[k], mrg_r.at[k], x, to).start()
    own_m = pltpu.make_async_copy(mout.at[r], mbuf.at[r], loc.at[1])
    own_m.start()
    own_m.wait()

    def hop(h, t):
        @pl.when(z - t >= 0)
        def _():
            z_copy(h, 0, t, own_rows(h), z - t).wait_recv()

            @pl.when(z < nz - 1)
            def _():
                z_copy(h, 0, t + 1, piece(h, z - t, c), z - t).start()

            w_sib(h, t, piece(h, z - t, c), z - t).start()

        @pl.when(z + t < nz)
        def _():
            z_copy(h, 1, t, own_rows(h), z + t).wait_recv()

            @pl.when(z > 0)
            def _():
                z_copy(h, 1, t + 1, piece(h, z + t, c), z + t).start()

            w_sib(h, nz - 1 + t, piece(h, z + t, c), z + t).start()

    hop(0, 1)
    if nz == 2:
        launch(1)
    for k in range(1, n):
        src = (r + n - k) % n
        rdma(mout.at[src], mbuf.at[src], mrg_s.at[k], mrg_r.at[k], x, sib).wait_recv()
    squares = jnp.zeros((rows_i, 1), jnp.float32)
    for s in range(n):
        v = mbuf[s].astype(jnp.float32)
        squares = squares + jnp.sum(v * v, axis=1, keepdims=True)
    inv = lax.rsqrt(squares / float(n * width) + 1e-06)
    for s in range(n):
        v = (mbuf[s].astype(jnp.float32) * inv * norm_gain[:, s * width : (s + 1) * width]).astype(jnp.bfloat16)
        spot = (s // 4) * 2 + s % 2
        for e in range(2):
            abuf[((s // 2) % 2) * 2 + e, 0:rows_i, spot * half : (spot + 1) * half] = v[:, e * half : (e + 1) * half]
    for d in range(1, 4):
        a_copy(d, 0, rows_i, ai_s, ai_r).start()

    for t in range(2, nz):
        hop(0, t)
        if t == max(nz - 2, 2):
            launch(1)

    def settled(h):
        own_w[h].wait()
        w_sib(h, 0, own_rows(h), z).wait_recv()
        for t in range(1, nz):
            @pl.when(z - t >= 0)
            def _():
                w_sib(h, t, own_rows(h), z - t).wait_recv()

            @pl.when(z + t < nz)
            def _():
                w_sib(h, nz - 1 + t, own_rows(h), z + t).wait_recv()

    def c_copy(d, j):
        _, ox, role = member(d)
        return rdma(csend.at[d - 1, j], crecv.at[d - 1, j], c_s.at[d - 1, j], c_r.at[d - 1, j], ox, role)

    parts = kv_width // CHUNK

    def partials(j):
        for d in (3, 1, 2):
            csend[d - 1, j] = jnp.dot(
                arecv[d - 1], wq[:, j * CHUNK : (j + 1) * CHUNK], preferred_element_type=jnp.float32
            ).astype(jnp.bfloat16)
            c_copy(d, j).start()

    def own_partial(j):
        cols = slice(j * CHUNK, (j + 1) * CHUNK)
        projected[:, cols] = jnp.dot(abuf[mine], wq[:, cols], preferred_element_type=jnp.float32)

    def add_partials(j):
        cols = slice(j * CHUNK, (j + 1) * CHUNK)
        for d in range(1, 4):
            c_copy(d, j).wait()
        projected[:, cols] = (
            projected[:, cols]
            + crecv[0, j].astype(jnp.float32)
            + crecv[1, j].astype(jnp.float32)
            + crecv[2, j].astype(jnp.float32)
        )

    for d in range(1, 4):
        a_copy(d, rows_i, rows_t, at_s, at_r).wait()
        a_copy(d, 0, rows_i, ai_s, ai_r).wait()
    settled(0)
    early = range(parts // 2)
    late = range(parts // 2, parts)
    hops = list(range(1, nz))
    for j in early:
        partials(j)
        if hops:
            hop(1, hops.pop(0))
    if hops:
        hop(1, hops.pop(0))
    for j in early:
        own_partial(j)
    for t in hops:
        hop(1, t)
    settled(1)
    for j in late:
        partials(j)
    for j in late:
        own_partial(j)
    for j in range(parts):
        add_partials(j)

    for k in range(1, chips):
        img_copy(k).wait_send()
    for k in range(chips):
        rdma(payload, ibuf.at[r], sib_s.at[k], sib_r.at[k], x, sib).wait_send()
    for k in range(1, n):
        rdma(mout.at[r], mbuf.at[r], mrg_s.at[k], mrg_r.at[k], x, sib).wait_send()
    for h in range(2):
        w_sib(h, 0, own_rows(h), z).wait_send()
        for t in range(1, nz):
            @pl.when((z - t + 1 >= 0) & (z < nz - 1))
            def _():
                z_copy(h, 0, t, own_rows(h), z).wait_send()

            @pl.when((z + t - 1 < nz) & (z > 0))
            def _():
                z_copy(h, 1, t, own_rows(h), z).wait_send()

            @pl.when(z - t >= 0)
            def _():
                w_sib(h, t, own_rows(h), z).wait_send()

            @pl.when(z + t < nz)
            def _():
                w_sib(h, nz - 1 + t, own_rows(h), z).wait_send()


def front(payload, vis_gain, w_merge, text, norm_gain, w_kv):
    n = lax.axis_size("role")
    nz = n // 4
    chips = n // 2
    width = w_merge.shape[1]
    vis = vis_gain.shape[0]
    model = norm_gain.shape[0]
    rows_i = IMGCAP * IMG_TOK
    length = text.shape[0] + rows_i
    kv_width = w_kv.shape[1]
    parts = kv_width // CHUNK
    bf = jnp.bfloat16
    dma = pltpu.SemaphoreType.DMA
    vmem = pl.BlockSpec(memory_space=pltpu.VMEM)
    hbm = pl.BlockSpec(memory_space=pl.ANY)
    return pl.pallas_call(
        functools.partial(front_kernel, n),
        out_shape=(
            jax.ShapeDtypeStruct((length, kv_width), jnp.float32),
            jax.ShapeDtypeStruct((n, 16, payload.shape[1] - vis), bf),
        ),
        in_specs=[hbm, vmem, hbm, vmem, vmem, hbm],
        out_specs=(vmem, vmem),
        scratch_shapes=[
            pltpu.VMEM((n,) + payload.shape, bf),
            pltpu.VMEM(w_merge.shape, bf),
            pltpu.VMEM((n * 16, vis), bf),
            pltpu.VMEM((n, rows_i, width), bf),
            pltpu.VMEM((n, rows_i, width), bf),
            pltpu.VMEM((4, length, model // 4), bf),
            pltpu.VMEM((3, length, model // 4), bf),
            pltpu.VMEM((model // 4, kv_width), bf),
            pltpu.VMEM((3, parts, length, CHUNK), bf),
            pltpu.VMEM((3, parts, length, CHUNK), bf),
            dma((chips,)), dma((chips,)), dma((chips,)), dma((chips,)),
            dma((n,)), dma((n,)), dma((3,)), dma((3,)), dma((3,)), dma((3,)),
            dma((2, 2, nz + 1)), dma((2, 2, nz + 1)), dma((2, 2 * nz)), dma((2, 2 * nz)),
            dma((3, parts)), dma((3, parts)), dma((4,)),
        ],
        compiler_params=pltpu.CompilerParams(
            collective_id=0, has_side_effects=True, vmem_limit_bytes=56 * 1024 * 1024
        ),
        name="front",
    )(payload, vis_gain[None, :], w_merge, text, norm_gain[None, :], w_kv)


def tail(
    projected, every_query, counts, targets,
    new_query, new_kv, text_len, block_dest, past_cache, past_scale, past_owner,
):
    rank_count = lax.axis_size("role")
    myself = lax.axis_index("role")
    groups = H // KVH
    factor = 1.0 / math.sqrt(HD)
    highest_prec = lax.Precision.HIGHEST
    bf = jnp.bfloat16
    length, kv_width = projected.shape
    chosen = (targets[:, None] == jnp.arange(rank_count)[None, :]).astype(jnp.int32)
    before = jnp.sum((jnp.cumsum(chosen, axis=0) - chosen) * chosen, axis=1)
    slot_of = targets * IMGCAP + before
    is_mine = slot_of[None, :] == myself * IMGCAP + jnp.arange(IMGCAP)[:, None]
    slot_count = jnp.sum(jnp.where(is_mine, counts[None, :], 0), axis=1)
    image_valid = (jnp.arange(IMG_TOK)[None, :] < slot_count[:, None]).reshape(-1)
    text_valid = jnp.arange(length - IMGCAP * IMG_TOK) < text_len[0]
    key_valid = jnp.concatenate([image_valid, text_valid])
    quantized, scales = quantize(projected)
    blocks = length // BLK
    per_rank = blocks // rank_count + 1
    block_target = block_dest[:, 0]
    chosen_block = (block_target[:, None] == jnp.arange(rank_count)[None, :]).astype(jnp.int32)
    before_block = jnp.sum((jnp.cumsum(chosen_block, axis=0) - chosen_block) * chosen_block, axis=1)
    page_of = block_target * per_rank + before_block
    routing = (page_of[None, :] == jnp.arange(rank_count * per_rank)[:, None]).astype(bf)
    send_quant = jnp.dot(
        routing, quantized.reshape(blocks, BLK * kv_width), preferred_element_type=jnp.float32
    )
    send_quant = send_quant.astype(bf).reshape(rank_count, per_rank, BLK, kv_width)
    small = jnp.concatenate([scales, key_valid.reshape(blocks, BLK).astype(bf)], axis=1)
    send_small = (
        jnp.dot(routing, small, preferred_element_type=jnp.float32)
        .astype(bf)
        .reshape(rank_count, per_rank, 2 * KVH + BLK)
    )
    kv_cache, got_small = (
        lax.all_to_all(send_quant, "role", split_axis=0, concat_axis=0, tiled=True),
        lax.all_to_all(send_small, "role", split_axis=0, concat_axis=0, tiled=True),
    )
    cache_scale, cache_valid = got_small[..., : 2 * KVH], got_small[..., 2 * KVH :]
    query = every_query.reshape(rank_count, KVH, groups, HD)

    past_pages = past_cache.shape[0]
    owner_hot = past_owner[:, 0][:, None] == jnp.arange(rank_count)[None, :]
    past_stack = past_cache.reshape(past_pages, BLK, 2, KVH, HD)
    past_factor = past_scale.astype(jnp.float32).reshape(past_pages, 2, KVH)[..., None, None]
    page_query = jnp.dot(
        owner_hot.astype(bf), every_query, preferred_element_type=jnp.float32
    ).astype(bf).reshape(past_pages, KVH, groups, HD)
    page_scores = (
        jnp.einsum("pbkd,pkgd->pkgb", past_stack[:, :, 0], page_query, preferred_element_type=jnp.float32)
        * past_factor[:, 0]
        * factor
    )
    page_top = jnp.max(page_scores, axis=3)
    page_weights = jnp.exp(page_scores - page_top[..., None])
    page_sum_w = jnp.sum(page_weights, axis=3)
    page_summed = jnp.einsum(
        "pkgb,pbkd->pkgd", (page_weights * past_factor[:, 1]).astype(bf), past_stack[:, :, 1],
        preferred_element_type=jnp.float32,
    )
    owned_mask = owner_hot[:, :, None, None]
    masked_top = jnp.where(owned_mask, page_top[:, None], -1e30)
    past_top = jnp.max(masked_top, axis=0)
    page_factor = jnp.where(owned_mask, jnp.exp(masked_top - past_top[None]), 0.0)
    past_total = jnp.sum(page_factor * page_sum_w[:, None], axis=0)
    past_summed = jnp.einsum("prkg,pkgd->rkgd", page_factor, page_summed, precision=highest_prec)

    stacked = kv_cache.reshape(rank_count, per_rank, BLK, 2, KVH, HD)
    in_factor = cache_scale.astype(jnp.float32).reshape(rank_count, per_rank, 2, KVH)
    key_factor = jnp.transpose(in_factor[:, :, 0], (0, 2, 1))[:, :, None, :, None]
    value_factor = jnp.transpose(in_factor[:, :, 1], (0, 2, 1))[:, :, None, :, None]
    scores = (
        jnp.einsum("scbkd,skgd->skgcb", stacked[:, :, :, 0], query, preferred_element_type=jnp.float32)
        * key_factor
        * factor
    )
    present = cache_valid.astype(jnp.float32)[:, None, None] > 0.5
    scores = jnp.where(present, scores, -1e30)
    highest = jnp.max(scores, axis=(3, 4))
    weights = jnp.where(present, jnp.exp(scores - highest[..., None, None]), 0.0)
    total_sum = jnp.sum(weights, axis=(3, 4))
    summed = jnp.einsum(
        "skgcb,scbkd->skgd", (weights * value_factor).astype(bf), stacked[:, :, :, 1],
        preferred_element_type=jnp.float32,
    )
    highest, total_sum, summed = combine(
        (highest, total_sum, summed), (past_top, past_total, past_summed)
    )
    packed = jnp.concatenate(
        [
            summed.reshape(rank_count, H, HD),
            jnp.concatenate(
                [highest.reshape(rank_count, 1, H), total_sum.reshape(rank_count, 1, H)], axis=2
            ),
        ],
        axis=1,
    )
    got = lax.all_to_all(packed, "role", split_axis=0, concat_axis=0, tiled=True)
    tops, totals, sums = got[:, H, :H], got[:, H, H : 2 * H], got[:, :H]
    fresh_vals = new_kv[0].astype(jnp.float32).reshape(2, KVH, HD)
    own_query = new_query[0].astype(jnp.float32).reshape(KVH, groups, HD)
    own_score = (jnp.sum(fresh_vals[0][:, None] * own_query, axis=2) * factor).reshape(H)
    final_top = jnp.maximum(jnp.max(tops, axis=0), own_score)
    old_factor = jnp.exp(tops - final_top)
    own_weight = jnp.exp(own_score - final_top)
    final_total = jnp.sum(totals * old_factor, axis=0) + own_weight
    own_value = jnp.repeat(fresh_vals[1], groups, axis=0)
    final_summed = jnp.sum(sums * old_factor[..., None], axis=0) + own_weight[:, None] * own_value
    attended = (final_summed / final_total[:, None]).reshape(1, H * HD).astype(bf)
    return (
        kv_cache.reshape(rank_count * per_rank, BLK, kv_width),
        cache_scale.reshape(rank_count * per_rank, 2 * KVH),
        attended,
    )


def plain_front(images, vis_gain, w_merge, prompt_text, norm_gain, w_kv, targets):
    rank_count = lax.axis_size("role")
    columns = w_merge.shape[1]
    normed_img = normalize(lax.all_gather(images, "role", axis=0, tiled=True), vis_gain).astype(
        jnp.bfloat16
    )
    merged = jnp.dot(normed_img, w_merge, preferred_element_type=jnp.float32).astype(jnp.bfloat16)
    image_total = targets.shape[0]
    chosen = (targets[:, None] == jnp.arange(rank_count)[None, :]).astype(jnp.int32)
    before = jnp.sum((jnp.cumsum(chosen, axis=0) - chosen) * chosen, axis=1)
    slot_of = targets * IMGCAP + before
    placing = (slot_of[None, :] == jnp.arange(rank_count * IMGCAP)[:, None]).astype(jnp.bfloat16)
    outgoing = jnp.dot(
        placing, merged.reshape(image_total, IMG_TOK * columns), preferred_element_type=jnp.float32
    )
    outgoing = outgoing.astype(jnp.bfloat16).reshape(rank_count, IMGCAP * IMG_TOK, columns)
    arrived = lax.all_to_all(outgoing, "role", split_axis=0, concat_axis=2, tiled=True)
    image_part = arrived.reshape(IMGCAP * IMG_TOK, rank_count * columns)
    sequence = jnp.concatenate([image_part, prompt_text], axis=0)
    normed = normalize(sequence, norm_gain).astype(jnp.bfloat16)
    rows = lax.all_gather(w_kv, "role", axis=0, tiled=True)
    return jnp.dot(normed, rows, preferred_element_type=jnp.float32)


def body(
    paired,
    images,
    vis_gain,
    w_merge,
    prompt_text,
    norm_gain,
    w_kv,
    new_query,
    new_kv,
    text_len,
    img_count,
    img_dest,
    block_dest,
    past_cache,
    past_scale,
    past_owner,
):
    n = lax.axis_size("role")
    if paired and images.shape[0] == 2 * IMG_TOK:
        meta = jnp.concatenate([img_dest[:, 0], img_count]).astype(jnp.bfloat16)
        meta = jnp.pad(meta, (0, 12))[:, None] * jnp.ones((1, 128), jnp.bfloat16)
        payload = jnp.concatenate([images, new_query.reshape(16, -1), meta], axis=1)
        projected, extras = front(payload, vis_gain, w_merge, prompt_text, norm_gain, w_kv)
        every_query = extras[:, :, :-128].reshape(n, -1)
        numbers = extras[:, :4, -1].astype(jnp.int32)
        targets = numbers[:, :2].reshape(-1)
        counts = numbers[:, 2:].reshape(-1)
    else:
        counts, targets = (
            lax.all_gather(img_count, "role", axis=0, tiled=True),
            lax.all_gather(img_dest[:, 0], "role", axis=0, tiled=True),
        )
        every_query = lax.all_gather(new_query, "role", axis=0, tiled=True)
        projected = plain_front(images, vis_gain, w_merge, prompt_text, norm_gain, w_kv, targets)
    return tail(
        projected, every_query, counts, targets,
        new_query, new_kv, text_len, block_dest, past_cache, past_scale, past_owner,
    )


def solution(mesh):
    in_specs = (
        P(("outer", "role"), None),
        P(),
        P(None, "role"),
        P(("outer", "role"), None),
        P(),
        P("role", None),
        P(("outer", "role"), None),
        P(("outer", "role"), None),
        P(("outer", "role")),
        P(("outer", "role")),
        P(("outer", "role"), None),
        P(("outer", "role"), None),
        P(("outer", "role"), None, None),
        P(("outer", "role"), None),
        P(("outer", "role"), None),
    )
    out_specs = (
        P(("outer", "role"), None, None),
        P(("outer", "role"), None),
        P(("outer", "role"), None),
    )
    paired = mesh.shape["outer"] == 2 and mesh.shape["role"] % 8 == 0
    return jax.shard_map(
        functools.partial(body, paired), mesh=mesh, in_specs=in_specs, out_specs=out_specs, check_vma=False
    )
```

```python
import functools
import math

import jax
import jax.numpy as jnp
from jax import lax
from jax.experimental import pallas as pl
from jax.experimental.pallas import tpu as pltpu
from jax.sharding import PartitionSpec as P

H = 64
KVH = 8
HD = 128
IMG_TOK = 8
IMGCAP = 4
BLK = 16


MESH = pl.DeviceIdType.MESH
CHUNK = 512


def normalize(values, gain_vec):
    values = values.astype(jnp.float32)
    return values * lax.rsqrt(jnp.mean(values * values, axis=-1, keepdims=True) + 1e-06) * gain_vec


def rotate(key_part):
    halfway = HD // 2
    position = jnp.arange(key_part.shape[0]).astype(jnp.float32)
    inverse = jnp.exp(jnp.arange(halfway).astype(jnp.float32) * (-2.0 * math.log(1000000.0) / HD))
    angles = position[:, None] * inverse[None, :]
    cosine = jnp.cos(angles)[:, None, :]
    sine_part = jnp.sin(angles)[:, None, :]
    front_half = key_part[..., :halfway]
    back_half = key_part[..., halfway:]
    return jnp.concatenate(
        [front_half * cosine - back_half * sine_part, back_half * cosine + front_half * sine_part],
        axis=-1,
    )


def quantize(projected):
    length = projected.shape[0]
    key_part = rotate(projected[:, : KVH * HD].reshape(length, KVH, HD))
    value_part = projected[:, KVH * HD :].reshape(length, KVH, HD)
    stacked = jnp.stack([key_part, value_part], axis=1).reshape(length // BLK, BLK, 2, KVH, HD)
    largest = jnp.max(jnp.abs(stacked), axis=(1, 4))
    scales = ((largest + 1e-05) / 448.0).astype(jnp.bfloat16)
    quantized = (stacked / scales.astype(jnp.float32)[:, None, :, :, None]).astype(jnp.bfloat16)
    return (
        quantized.reshape(length // BLK, BLK, 2 * KVH * HD),
        scales.reshape(length // BLK, 2 * KVH),
    )


def combine(earlier, later):
    left_top, left_total, left_summed = earlier
    right_top, right_total, right_summed = later
    highest = jnp.maximum(left_top, right_top)
    left_factor = jnp.exp(left_top - highest)
    right_factor = jnp.exp(right_top - highest)
    return (
        highest,
        left_total * left_factor + right_total * right_factor,
        left_summed * left_factor[..., None] + right_summed * right_factor[..., None],
    )


def front_kernel(
    n, payload, vis_gain, w_merge, text, norm_gain, w_kv,
    projected, extras,
    ibuf, wm, nimg, mout, mbuf, abuf, arecv, wq, csend, crecv,
    img_s, img_r, sib_s, sib_r, mrg_s, mrg_r, at_s, at_r, ai_s, ai_r,
    z_s, z_r, ws_s, ws_r, c_s, c_r, loc,
):
    nz = n // 4
    chips = n // 2
    vis = vis_gain.shape[1]
    x = lax.axis_index("outer")
    r = lax.axis_index("role")
    z = r // 4
    y = (r // 2) % 2
    c = r % 2
    q = r // 2
    sib = q * 2 + (1 - c)
    width = w_merge.shape[1]
    half = width // 2
    rows_t = text.shape[0]
    rows_i = IMGCAP * IMG_TOK
    mine = y * 2 + x

    def rdma(src, dst, ss, rs, outer, role):
        return pltpu.make_async_remote_copy(
            src_ref=src, dst_ref=dst, send_sem=ss, recv_sem=rs,
            device_id=(outer, role), device_id_type=MESH,
        )

    def member(d):
        dx, dy = d % 2, d // 2
        ox, oy = (x + dx) % 2, (y + dy) % 2
        return oy * 2 + ox, ox, z * 4 + oy * 2 + c

    barrier = pltpu.get_barrier_semaphore()
    for k in range(1, n):
        pl.semaphore_signal(barrier, inc=1, device_id=(x, (r + k) % n), device_id_type=MESH)
    for d in (1, 3):
        _, ox, role = member(d)
        pl.semaphore_signal(barrier, inc=1, device_id=(ox, role), device_id_type=MESH)
    wm_copy = pltpu.make_async_copy(w_merge, wm, loc.at[0])
    wm_copy.start()
    pl.semaphore_wait(barrier, n + 1)

    def img_copy(k):
        slot = ibuf.at[r]
        return rdma(payload, slot, img_s.at[k], img_r.at[k], x, ((q + k) % chips) * 2 + c)

    for k in range(1, chips):
        img_copy(k).start()
    rdma(payload, ibuf.at[r], sib_s.at[0], sib_r.at[0], x, sib).start()
    own_img = pltpu.make_async_copy(payload, ibuf.at[r], loc.at[1])
    own_img.start()

    kv_width = w_kv.shape[1]
    side = CHUNK
    parts = kv_width // CHUNK

    def piece(h, zz, core):
        at = pl.multiple_of((zz * 2 + core) * half, half)
        return wq.at[pl.ds(at, half), h * side : (h + 1) * side]

    def own_rows(h):
        return w_kv.at[pl.ds(pl.multiple_of(x * half, half), half), h * side : (h + 1) * side]

    own_w = [pltpu.make_async_copy(own_rows(h), piece(h, z, c), loc.at[2 + h]) for h in range(parts)]

    def z_copy(h, way, t, src, zz):
        role = ((z + (1 if way == 0 else nz - 1)) % nz) * 4 + y * 2 + c
        return rdma(src, piece(h, zz, c), z_s.at[h, way, t], z_r.at[h, way, t], x, role)

    def w_sib(h, i, src, zz):
        return rdma(src, piece(h, zz, c), ws_s.at[h, i], ws_r.at[h, i], x, sib)

    def launch(h):
        @pl.when(z < nz - 1)
        def _():
            z_copy(h, 0, 1, own_rows(h), z).start()

        @pl.when(z > 0)
        def _():
            z_copy(h, 1, 1, own_rows(h), z).start()

        own_w[h].start()
        w_sib(h, 0, own_rows(h), z).start()

    launch(0)

    def norm_rows(i, carry):
        at = pl.multiple_of(i * 16, 16)
        v = text[pl.ds(at, 16), :].astype(jnp.float32)
        inv = lax.rsqrt(jnp.mean(v * v, axis=1, keepdims=True) + 1e-06)
        v = (v * inv * norm_gain[...]).astype(jnp.bfloat16)
        for g in range(4):
            for s in range(chips):
                col = (s // 2) * 4 * width + (g // 2) * 2 * width + (s % 2) * width + (g % 2) * half
                abuf[g, pl.ds(rows_i + at, 16), s * half : (s + 1) * half] = v[:, col : col + half]
        return carry

    lax.fori_loop(0, rows_t // 16, norm_rows, 0)

    def a_copy(d, lo, size, ss, rs):
        g, ox, role = member(d)
        return rdma(
            abuf.at[g, pl.ds(lo, size), :], arecv.at[d - 1, pl.ds(lo, size), :],
            ss.at[d - 1], rs.at[d - 1], ox, role,
        )

    for d in range(1, 4):
        a_copy(d, rows_i, rows_t, at_s, at_r).start()

    own_img.wait()
    for k in range(1, chips):
        src = ((q + chips - k) % chips) * 2 + c
        rdma(payload, ibuf.at[src], img_s.at[k], img_r.at[k], x, sib).wait_recv()
        rdma(ibuf.at[src], ibuf.at[src], sib_s.at[k], sib_r.at[k], x, sib).start()
    for k in range(chips):
        src = ((q + chips - k) % chips) * 2 + (1 - c)
        rdma(payload, ibuf.at[src], sib_s.at[k], sib_r.at[k], x, sib).wait_recv()

    def norm_images(i, carry):
        v = ibuf[i, :, :vis].astype(jnp.float32)
        inv = lax.rsqrt(jnp.mean(v * v, axis=1, keepdims=True) + 1e-06)
        nimg[pl.ds(pl.multiple_of(i * 16, 16), 16), :] = (v * inv * vis_gain[...]).astype(jnp.bfloat16)
        extras[i, :, :] = ibuf[i, :, vis:]
        return carry

    lax.fori_loop(0, n, norm_images, 0)
    wm_copy.wait()
    merged = jnp.dot(nimg[...], wm[...], preferred_element_type=jnp.float32).astype(jnp.bfloat16)

    images = 2 * n
    lane = lax.broadcasted_iota(jnp.int32, (1, images * IMG_TOK), 1)
    image = lane // IMG_TOK
    last = ibuf.shape[2]
    named = [
        jnp.concatenate(
            [ibuf[i // 2, i % 2 : i % 2 + 1, last - 128 :].astype(jnp.float32)] * (images * IMG_TOK // 128), axis=1
        )
        for i in range(images)
    ]
    target = jnp.zeros(lane.shape, jnp.float32)
    for i in range(images):
        target = jnp.where(image == i, named[i], target)
    place = target * float(IMGCAP)
    for i in range(images):
        place = place + jnp.where((image > i) & (named[i] == target), 1.0, 0.0)
    row = lax.broadcasted_iota(jnp.int32, (n * rows_i, images * IMG_TOK), 0)
    col = lax.broadcasted_iota(jnp.int32, (n * rows_i, images * IMG_TOK), 1)
    hot = ((row // IMG_TOK).astype(jnp.float32) == place) & (row % IMG_TOK == col % IMG_TOK)
    placed = jnp.dot(
        jnp.where(hot, 1.0, 0.0).astype(jnp.bfloat16), merged, preferred_element_type=jnp.float32
    ).astype(jnp.bfloat16)
    for p in range(n):
        mout[p] = placed[p * rows_i : (p + 1) * rows_i]
    for k in range(1, n):
        to = (r + k) % n
        rdma(mout.at[to], mbuf.at[r], mrg_s.at[k], mrg_r.at[k], x, to).start()
    own_m = pltpu.make_async_copy(mout.at[r], mbuf.at[r], loc.at[1])
    own_m.start()
    own_m.wait()

    def hop(h, t):
        @pl.when(z - t >= 0)
        def _():
            z_copy(h, 0, t, own_rows(h), z - t).wait_recv()

            @pl.when(z < nz - 1)
            def _():
                z_copy(h, 0, t + 1, piece(h, z - t, c), z - t).start()

            w_sib(h, t, piece(h, z - t, c), z - t).start()

        @pl.when(z + t < nz)
        def _():
            z_copy(h, 1, t, own_rows(h), z + t).wait_recv()

            @pl.when(z > 0)
            def _():
                z_copy(h, 1, t + 1, piece(h, z + t, c), z + t).start()

            w_sib(h, nz - 1 + t, piece(h, z + t, c), z + t).start()

    hop(0, 1)
    launch(1)
    for k in range(1, n):
        src = (r + n - k) % n
        rdma(mout.at[src], mbuf.at[src], mrg_s.at[k], mrg_r.at[k], x, sib).wait_recv()
    squares = jnp.zeros((rows_i, 1), jnp.float32)
    for s in range(n):
        v = mbuf[s].astype(jnp.float32)
        squares = squares + jnp.sum(v * v, axis=1, keepdims=True)
    inv = lax.rsqrt(squares / float(n * width) + 1e-06)
    for s in range(n):
        v = (mbuf[s].astype(jnp.float32) * inv * norm_gain[:, s * width : (s + 1) * width]).astype(jnp.bfloat16)
        spot = (s // 4) * 2 + s % 2
        for e in range(2):
            abuf[((s // 2) % 2) * 2 + e, 0:rows_i, spot * half : (spot + 1) * half] = v[:, e * half : (e + 1) * half]
    for d in range(1, 4):
        a_copy(d, 0, rows_i, ai_s, ai_r).start()

    for t in range(2, nz):
        hop(0, t)

    def settled(h):
        own_w[h].wait()
        w_sib(h, 0, own_rows(h), z).wait_recv()
        for t in range(1, nz):
            @pl.when(z - t >= 0)
            def _():
                w_sib(h, t, own_rows(h), z - t).wait_recv()

            @pl.when(z + t < nz)
            def _():
                w_sib(h, nz - 1 + t, own_rows(h), z + t).wait_recv()

    def c_copy(d, j):
        _, ox, role = member(d)
        return rdma(csend.at[d - 1, j], crecv.at[d - 1, j], c_s.at[d - 1, j], c_r.at[d - 1, j], ox, role)

    parts = kv_width // CHUNK

    def partials(j):
        for d in (3, 1, 2):
            csend[d - 1, j] = jnp.dot(
                arecv[d - 1], wq[:, j * CHUNK : (j + 1) * CHUNK], preferred_element_type=jnp.float32
            ).astype(jnp.bfloat16)
            c_copy(d, j).start()

    def own_partial(j):
        cols = slice(j * CHUNK, (j + 1) * CHUNK)
        projected[:, cols] = jnp.dot(abuf[mine], wq[:, cols], preferred_element_type=jnp.float32)

    def add_partials(j):
        cols = slice(j * CHUNK, (j + 1) * CHUNK)
        for d in range(1, 4):
            c_copy(d, j).wait()
        projected[:, cols] = (
            projected[:, cols]
            + crecv[0, j].astype(jnp.float32)
            + crecv[1, j].astype(jnp.float32)
            + crecv[2, j].astype(jnp.float32)
        )

    for d in range(1, 4):
        a_copy(d, rows_i, rows_t, at_s, at_r).wait()
        a_copy(d, 0, rows_i, ai_s, ai_r).wait()
    for h in range(parts):
        settled(h)
        partials(h)
        for t in range(1, nz):
            if t == nz - 1:
                own_partial(h)
            if h + 1 < parts:
                hop(h + 1, t)
                if t == 1 and h + 2 < parts:
                    launch(h + 2)
    for j in range(parts):
        add_partials(j)

    for k in range(1, chips):
        img_copy(k).wait_send()
    for k in range(chips):
        rdma(payload, ibuf.at[r], sib_s.at[k], sib_r.at[k], x, sib).wait_send()
    for k in range(1, n):
        rdma(mout.at[r], mbuf.at[r], mrg_s.at[k], mrg_r.at[k], x, sib).wait_send()
    for h in range(parts):
        w_sib(h, 0, own_rows(h), z).wait_send()
        for t in range(1, nz):
            @pl.when((z - t + 1 >= 0) & (z < nz - 1))
            def _():
                z_copy(h, 0, t, own_rows(h), z).wait_send()

            @pl.when((z + t - 1 < nz) & (z > 0))
            def _():
                z_copy(h, 1, t, own_rows(h), z).wait_send()

            @pl.when(z - t >= 0)
            def _():
                w_sib(h, t, own_rows(h), z).wait_send()

            @pl.when(z + t < nz)
            def _():
                w_sib(h, nz - 1 + t, own_rows(h), z).wait_send()


def front(payload, vis_gain, w_merge, text, norm_gain, w_kv):
    n = lax.axis_size("role")
    nz = n // 4
    chips = n // 2
    width = w_merge.shape[1]
    vis = vis_gain.shape[0]
    model = norm_gain.shape[0]
    rows_i = IMGCAP * IMG_TOK
    length = text.shape[0] + rows_i
    kv_width = w_kv.shape[1]
    parts = kv_width // CHUNK
    bf = jnp.bfloat16
    dma = pltpu.SemaphoreType.DMA
    vmem = pl.BlockSpec(memory_space=pltpu.VMEM)
    hbm = pl.BlockSpec(memory_space=pl.ANY)
    return pl.pallas_call(
        functools.partial(front_kernel, n),
        out_shape=(
            jax.ShapeDtypeStruct((length, kv_width), jnp.float32),
            jax.ShapeDtypeStruct((n, 16, payload.shape[1] - vis), bf),
        ),
        in_specs=[hbm, vmem, hbm, vmem, vmem, hbm],
        out_specs=(vmem, vmem),
        scratch_shapes=[
            pltpu.VMEM((n,) + payload.shape, bf),
            pltpu.VMEM(w_merge.shape, bf),
            pltpu.VMEM((n * 16, vis), bf),
            pltpu.VMEM((n, rows_i, width), bf),
            pltpu.VMEM((n, rows_i, width), bf),
            pltpu.VMEM((4, length, model // 4), bf),
            pltpu.VMEM((3, length, model // 4), bf),
            pltpu.VMEM((model // 4, kv_width), bf),
            pltpu.VMEM((3, parts, length, CHUNK), bf),
            pltpu.VMEM((3, parts, length, CHUNK), bf),
            dma((chips,)), dma((chips,)), dma((chips,)), dma((chips,)),
            dma((n,)), dma((n,)), dma((3,)), dma((3,)), dma((3,)), dma((3,)),
            dma((parts, 2, nz + 1)), dma((parts, 2, nz + 1)), dma((parts, 2 * nz)), dma((parts, 2 * nz)),
            dma((3, parts)), dma((3, parts)), dma((2 + parts,)),
        ],
        compiler_params=pltpu.CompilerParams(
            collective_id=0, has_side_effects=True, vmem_limit_bytes=56 * 1024 * 1024
        ),
        name="front",
    )(payload, vis_gain[None, :], w_merge, text, norm_gain[None, :], w_kv)


def tail(
    projected, every_query, counts, targets,
    new_query, new_kv, text_len, block_dest, past_cache, past_scale, past_owner,
):
    rank_count = lax.axis_size("role")
    myself = lax.axis_index("role")
    groups = H // KVH
    factor = 1.0 / math.sqrt(HD)
    highest_prec = lax.Precision.HIGHEST
    bf = jnp.bfloat16
    length, kv_width = projected.shape
    chosen = (targets[:, None] == jnp.arange(rank_count)[None, :]).astype(jnp.int32)
    before = jnp.sum((jnp.cumsum(chosen, axis=0) - chosen) * chosen, axis=1)
    slot_of = targets * IMGCAP + before
    is_mine = slot_of[None, :] == myself * IMGCAP + jnp.arange(IMGCAP)[:, None]
    slot_count = jnp.sum(jnp.where(is_mine, counts[None, :], 0), axis=1)
    image_valid = (jnp.arange(IMG_TOK)[None, :] < slot_count[:, None]).reshape(-1)
    text_valid = jnp.arange(length - IMGCAP * IMG_TOK) < text_len[0]
    key_valid = jnp.concatenate([image_valid, text_valid])
    quantized, scales = quantize(projected)
    blocks = length // BLK
    per_rank = blocks // rank_count + 1
    block_target = block_dest[:, 0]
    chosen_block = (block_target[:, None] == jnp.arange(rank_count)[None, :]).astype(jnp.int32)
    before_block = jnp.sum((jnp.cumsum(chosen_block, axis=0) - chosen_block) * chosen_block, axis=1)
    page_of = block_target * per_rank + before_block
    routing = (page_of[None, :] == jnp.arange(rank_count * per_rank)[:, None]).astype(bf)
    send_quant = jnp.dot(
        routing, quantized.reshape(blocks, BLK * kv_width), preferred_element_type=jnp.float32
    )
    send_quant = send_quant.astype(bf).reshape(rank_count, per_rank, BLK, kv_width)
    small = jnp.concatenate([scales, key_valid.reshape(blocks, BLK).astype(bf)], axis=1)
    send_small = (
        jnp.dot(routing, small, preferred_element_type=jnp.float32)
        .astype(bf)
        .reshape(rank_count, per_rank, 2 * KVH + BLK)
    )
    kv_cache, got_small = (
        lax.all_to_all(send_quant, "role", split_axis=0, concat_axis=0, tiled=True),
        lax.all_to_all(send_small, "role", split_axis=0, concat_axis=0, tiled=True),
    )
    cache_scale, cache_valid = got_small[..., : 2 * KVH], got_small[..., 2 * KVH :]
    query = every_query.reshape(rank_count, KVH, groups, HD)

    past_pages = past_cache.shape[0]
    owner_hot = past_owner[:, 0][:, None] == jnp.arange(rank_count)[None, :]
    past_stack = past_cache.reshape(past_pages, BLK, 2, KVH, HD)
    past_factor = past_scale.astype(jnp.float32).reshape(past_pages, 2, KVH)[..., None, None]
    page_query = jnp.dot(
        owner_hot.astype(bf), every_query, preferred_element_type=jnp.float32
    ).astype(bf).reshape(past_pages, KVH, groups, HD)
    page_scores = (
        jnp.einsum("pbkd,pkgd->pkgb", past_stack[:, :, 0], page_query, preferred_element_type=jnp.float32)
        * past_factor[:, 0]
        * factor
    )
    page_top = jnp.max(page_scores, axis=3)
    page_weights = jnp.exp(page_scores - page_top[..., None])
    page_sum_w = jnp.sum(page_weights, axis=3)
    page_summed = jnp.einsum(
        "pkgb,pbkd->pkgd", (page_weights * past_factor[:, 1]).astype(bf), past_stack[:, :, 1],
        preferred_element_type=jnp.float32,
    )
    owned_mask = owner_hot[:, :, None, None]
    masked_top = jnp.where(owned_mask, page_top[:, None], -1e30)
    past_top = jnp.max(masked_top, axis=0)
    page_factor = jnp.where(owned_mask, jnp.exp(masked_top - past_top[None]), 0.0)
    past_total = jnp.sum(page_factor * page_sum_w[:, None], axis=0)
    past_summed = jnp.einsum("prkg,pkgd->rkgd", page_factor, page_summed, precision=highest_prec)

    stacked = kv_cache.reshape(rank_count, per_rank, BLK, 2, KVH, HD)
    in_factor = cache_scale.astype(jnp.float32).reshape(rank_count, per_rank, 2, KVH)
    key_factor = jnp.transpose(in_factor[:, :, 0], (0, 2, 1))[:, :, None, :, None]
    value_factor = jnp.transpose(in_factor[:, :, 1], (0, 2, 1))[:, :, None, :, None]
    scores = (
        jnp.einsum("scbkd,skgd->skgcb", stacked[:, :, :, 0], query, preferred_element_type=jnp.float32)
        * key_factor
        * factor
    )
    present = cache_valid.astype(jnp.float32)[:, None, None] > 0.5
    scores = jnp.where(present, scores, -1e30)
    highest = jnp.max(scores, axis=(3, 4))
    weights = jnp.where(present, jnp.exp(scores - highest[..., None, None]), 0.0)
    total_sum = jnp.sum(weights, axis=(3, 4))
    summed = jnp.einsum(
        "skgcb,scbkd->skgd", (weights * value_factor).astype(bf), stacked[:, :, :, 1],
        preferred_element_type=jnp.float32,
    )
    highest, total_sum, summed = combine(
        (highest, total_sum, summed), (past_top, past_total, past_summed)
    )
    packed = jnp.concatenate(
        [
            summed.reshape(rank_count, H, HD),
            jnp.concatenate(
                [highest.reshape(rank_count, 1, H), total_sum.reshape(rank_count, 1, H)], axis=2
            ),
        ],
        axis=1,
    )
    got = lax.all_to_all(packed, "role", split_axis=0, concat_axis=0, tiled=True)
    tops, totals, sums = got[:, H, :H], got[:, H, H : 2 * H], got[:, :H]
    fresh_vals = new_kv[0].astype(jnp.float32).reshape(2, KVH, HD)
    own_query = new_query[0].astype(jnp.float32).reshape(KVH, groups, HD)
    own_score = (jnp.sum(fresh_vals[0][:, None] * own_query, axis=2) * factor).reshape(H)
    final_top = jnp.maximum(jnp.max(tops, axis=0), own_score)
    old_factor = jnp.exp(tops - final_top)
    own_weight = jnp.exp(own_score - final_top)
    final_total = jnp.sum(totals * old_factor, axis=0) + own_weight
    own_value = jnp.repeat(fresh_vals[1], groups, axis=0)
    final_summed = jnp.sum(sums * old_factor[..., None], axis=0) + own_weight[:, None] * own_value
    attended = (final_summed / final_total[:, None]).reshape(1, H * HD).astype(bf)
    return (
        kv_cache.reshape(rank_count * per_rank, BLK, kv_width),
        cache_scale.reshape(rank_count * per_rank, 2 * KVH),
        attended,
    )


def plain_front(images, vis_gain, w_merge, prompt_text, norm_gain, w_kv, targets):
    rank_count = lax.axis_size("role")
    columns = w_merge.shape[1]
    normed_img = normalize(lax.all_gather(images, "role", axis=0, tiled=True), vis_gain).astype(
        jnp.bfloat16
    )
    merged = jnp.dot(normed_img, w_merge, preferred_element_type=jnp.float32).astype(jnp.bfloat16)
    image_total = targets.shape[0]
    chosen = (targets[:, None] == jnp.arange(rank_count)[None, :]).astype(jnp.int32)
    before = jnp.sum((jnp.cumsum(chosen, axis=0) - chosen) * chosen, axis=1)
    slot_of = targets * IMGCAP + before
    placing = (slot_of[None, :] == jnp.arange(rank_count * IMGCAP)[:, None]).astype(jnp.bfloat16)
    outgoing = jnp.dot(
        placing, merged.reshape(image_total, IMG_TOK * columns), preferred_element_type=jnp.float32
    )
    outgoing = outgoing.astype(jnp.bfloat16).reshape(rank_count, IMGCAP * IMG_TOK, columns)
    arrived = lax.all_to_all(outgoing, "role", split_axis=0, concat_axis=2, tiled=True)
    image_part = arrived.reshape(IMGCAP * IMG_TOK, rank_count * columns)
    sequence = jnp.concatenate([image_part, prompt_text], axis=0)
    normed = normalize(sequence, norm_gain).astype(jnp.bfloat16)
    rows = lax.all_gather(w_kv, "role", axis=0, tiled=True)
    return jnp.dot(normed, rows, preferred_element_type=jnp.float32)


def body(
    paired,
    images,
    vis_gain,
    w_merge,
    prompt_text,
    norm_gain,
    w_kv,
    new_query,
    new_kv,
    text_len,
    img_count,
    img_dest,
    block_dest,
    past_cache,
    past_scale,
    past_owner,
):
    n = lax.axis_size("role")
    if paired and images.shape[0] == 2 * IMG_TOK:
        meta = jnp.concatenate([img_dest[:, 0], img_count]).astype(jnp.bfloat16)
        meta = jnp.pad(meta, (0, 12))[:, None] * jnp.ones((1, 128), jnp.bfloat16)
        payload = jnp.concatenate([images, new_query.reshape(16, -1), meta], axis=1)
        projected, extras = front(payload, vis_gain, w_merge, prompt_text, norm_gain, w_kv)
        every_query = extras[:, :, :-128].reshape(n, -1)
        numbers = extras[:, :4, -1].astype(jnp.int32)
        targets = numbers[:, :2].reshape(-1)
        counts = numbers[:, 2:].reshape(-1)
    else:
        counts, targets = (
            lax.all_gather(img_count, "role", axis=0, tiled=True),
            lax.all_gather(img_dest[:, 0], "role", axis=0, tiled=True),
        )
        every_query = lax.all_gather(new_query, "role", axis=0, tiled=True)
        projected = plain_front(images, vis_gain, w_merge, prompt_text, norm_gain, w_kv, targets)
    return tail(
        projected, every_query, counts, targets,
        new_query, new_kv, text_len, block_dest, past_cache, past_scale, past_owner,
    )


def solution(mesh):
    in_specs = (
        P(("outer", "role"), None),
        P(),
        P(None, "role"),
        P(("outer", "role"), None),
        P(),
        P("role", None),
        P(("outer", "role"), None),
        P(("outer", "role"), None),
        P(("outer", "role")),
        P(("outer", "role")),
        P(("outer", "role"), None),
        P(("outer", "role"), None),
        P(("outer", "role"), None, None),
        P(("outer", "role"), None),
        P(("outer", "role"), None),
    )
    out_specs = (
        P(("outer", "role"), None, None),
        P(("outer", "role"), None),
        P(("outer", "role"), None),
    )
    paired = mesh.shape["outer"] == 2 and mesh.shape["role"] % 8 == 0
    return jax.shard_map(
        functools.partial(body, paired), mesh=mesh, in_specs=in_specs, out_specs=out_specs, check_vma=False
    )
```
